32 devices in a mesh: groups: 1, dev: 8 (over z, y), side: 4 (over x, core).
Axes of the slice: x: 2, y: 2, z: 4, core: 2. Of those that a mesh axis runs over, the one named last changes fastest.
Arguments:
- queries: bfloat16 [256, 4096], P(('groups', 'dev', 'side')), may hold values from -160 to 160
- kv_cache: bfloat16 [256, 192, 1024], P(('groups', 'dev', 'side')), may hold values from -4 to 4
- new_kv: bfloat16 [256, 1024], P(('groups', 'dev', 'side')), may hold values from -4 to 4
- lengths: int32 [256], P(('groups', 'dev', 'side')), may hold values from 24 to 192, as said below
- residual: bfloat16 [256, 2048], P(('groups', 'dev', 'side')), may hold values from -36 to 36
- w_out: bfloat16 [4096, 2048], P('side'), may hold values from -0.59765625 to 0.59765625
- norm_gain: float32 [2048], replicated, may hold values from 0.5 to 1.5
- expert_ids: int32 [256, 8], P(('groups', 'dev', 'side')), may hold values from 0 to 15, all different within a row; in each aligned block of 8 rows (0 to 7, 8 to 15, ...) at most 8 rows name the same one
- route_level: int32 [256, 8], P(('groups', 'dev', 'side')), may hold values from 1 to 255
- w_in: bfloat16 [32, 2048, 768], P(('dev', 'side')), may hold values from -0.125 to 0.125
- w_down: bfloat16 [32, 384, 2048], P(('dev', 'side')), may hold values from -0.4375 to 0.4375
Outputs:
- stream: bfloat16 [256, 2048], P(('groups', 'dev', 'side'))
- expert_sum: bfloat16 [256, 2048], P(('groups', 'dev', 'side'))
The draws below stay inside these ranges and needn't reach their ends.
Inputs may be any that keep to these rules, and one draw needn't show every extreme that they name: `lengths`: in each aligned block of 8 requests some request has 192 cached tokens. `expert_ids`: A row names 8 different experts. In each aligned block of 8 rows no expert is named by more than 8 rows, and in some block some expert is named by exactly 8 rows.
All inputs are finite; a program needn't handle non-finite values.
Results may differ from the reference program's by a relative error of at most 0.013.
Values may be sent and summed in bfloat16 or wider, within the bound.
A program may use at most 64 MiB of HBM per device.

```python
import math
import jax
import jax.numpy as jnp
import numpy as np
from jax import lax

D = 2048
HQ = 32
KVH = 4
HD = 128
FF = 768
TOPK = 8
CACHE = 192
REQ_DEV = 8
REQ = 256
SHARDS = 32
EXPERTS = 16
FH = 384
MOST = 8


def attention_parts(key):
    base_key = jax.random.fold_in(key, 11)
    subkeys = jax.random.split(base_key, 2)
    kv_values = jnp.clip(jax.random.normal(subkeys[0], (REQ, CACHE, 2 * KVH * HD), jnp.float32), -4.0, 4.0)
    queries = jnp.clip(jax.random.normal(subkeys[1], (REQ, HQ * HD), jnp.float32), -4.0, 4.0)
    return (queries, kv_values)


def draw_queries(key, part):
    return attention_parts(key)[0].astype(jnp.bfloat16)


def draw_kv_cache(key, part):
    return attention_parts(key)[1].astype(jnp.bfloat16)


def draw_lengths(key, part):
    subkeys = jax.random.split(jax.random.fold_in(key, 31), 2)
    drawn = jax.random.randint(subkeys[0], (REQ,), CACHE // 8, CACHE + 1)
    longest = jax.random.randint(subkeys[1], (REQ // REQ_DEV,), 0, REQ_DEV)
    indices = jnp.arange(REQ)
    chosen = indices % REQ_DEV == jnp.repeat(longest, REQ_DEV, total_repeat_length=REQ)
    return jnp.where(chosen, CACHE, drawn).astype(jnp.int32)


def draw_residual(key, part):
    subkeys = jax.random.split(jax.random.fold_in(key, 23), 3)
    lower = math.log(0.3)
    upper = math.log(3.0)
    column_scale = jnp.exp(jax.random.uniform(subkeys[1], (D,), jnp.float32, lower, upper))
    row_scale = jnp.exp(jax.random.uniform(subkeys[2], (REQ,), jnp.float32, lower, upper))
    noise = jnp.clip(jax.random.normal(subkeys[0], (REQ, D), jnp.float32), -4.0, 4.0)
    return (noise * row_scale[:, None] * column_scale[None, :]).astype(jnp.bfloat16)


def with_ends(entries, own_key, smallest, largest):
    place = [jax.random.randint(jax.random.fold_in(own_key, axis), (), 0, length) for axis, length in enumerate(entries.shape)]
    widest = entries.shape.index(max(entries.shape))
    next_to = place[:widest] + [(place[widest] + 1) % entries.shape[widest]] + place[widest + 1:]
    return entries.at[tuple(place)].set(smallest).at[tuple(next_to)].set(largest)


def level_of(stream_key, extent, cuts, least, top_value):
    def one(dim, parts):
        heights = jax.random.uniform(jax.random.fold_in(jax.random.fold_in(stream_key, 6), dim), (parts,), jnp.float32, least / len(cuts), top_value / len(cuts))
        return jnp.repeat(jnp.exp(heights), extent[dim] // parts).reshape((-1,) + (1,) * (len(extent) - dim - 1))

    level = one(*cuts[0])
    for cut in cuts[1:]:
        level = level * one(*cut)
    return level


def routed_block(key, own, number, rows, amount, top, reach, slope):
    sequence = jax.random.permutation(key, amount)
    heavy_load, usual = load_shares(amount, rows * top, reach, slope, True), load_shares(amount, rows * top, reach, slope, False)
    places = jnp.arange(amount)

    def named(sizes, rotation):
        used = int((sizes > 0).sum())
        fixed = max(1, used // 4)
        shifted = fixed + (places - fixed + rotation * (used - fixed)) % max(1, amount - fixed)
        return jnp.zeros((amount,), jnp.int32).at[sequence[jnp.where(places < fixed, places, shifted)]].set(jnp.asarray(sizes, jnp.int32))

    sizes = jnp.where(number % 4 == 0, named(heavy_load, number // 4), named(usual, number - number // 4 - 1))
    mixed = jax.random.permutation(jax.random.fold_in(own, 3), amount)
    donor, receiver = mixed[0:amount // 2 * 2:2], mixed[1:amount // 2 * 2:2]
    room = jnp.minimum(sizes[donor] - 1, reach - sizes[receiver]) // 2
    room = jnp.where((donor == sequence[0]) | (receiver == sequence[0]) | (sizes[receiver] == 0), 0, jnp.maximum(room, 0))
    shifted = jax.random.randint(jax.random.fold_in(own, 4), (amount // 2,), 0, 1 << 20) % (room + 1)
    sizes = sizes.at[donor].add(-shifted).at[receiver].add(shifted)
    items = jnp.searchsorted(jnp.cumsum(sizes), jnp.arange(rows * top), side="right").astype(jnp.int32)
    grid = items.reshape(top, rows).T
    grid = grid[jax.random.permutation(jax.random.fold_in(own, 1), rows)]
    rotation = jax.random.randint(jax.random.fold_in(own, 2), (rows, 1), 0, top)
    return jnp.take_along_axis(grid, (jnp.arange(top)[None, :] + rotation) % top, axis=1)


def load_shares(count, total, limit, lean, full):
    weights = [(1 << 20) // math.isqrt(grade ** lean) + 1 for grade in range(1, count + 1)]
    largest = limit if full else min(limit, max(-(-total // count), total * weights[0] // sum(weights)))
    least = 1 if total - largest >= count - 1 else 0
    given, surplus = [largest] + [least] * (count - 1), total - largest - least * (count - 1)
    while surplus > 0:
        candidates = [i for i in range(1, count) if given[i] < largest] or [i for i in range(1, count) if given[i] < limit]
        mass, remaining = sum([weights[i] for i in candidates]), surplus
        for i in candidates:
            extra = min(limit - given[i], max(1, remaining * weights[i] // mass), surplus)
            given[i] = given[i] + extra
            surplus = surplus - extra
    return np.array(given)


def scatter_about(own_key, shape, spread, most, cuts=(), kind=jnp.bfloat16):
    result = spread * jax.random.normal(own_key, shape, jnp.float32)
    if cuts:
        result = result * level_of(own_key, shape, cuts, -0.22, 0.18)
    return jnp.clip(result, -most, most).astype(kind)


def setup_inputs(seed: int = 0, part: int = 0) -> dict:
    streams_of = jax.random.split(jax.random.key(seed), 12)
    part_splits = jax.random.split(jax.random.fold_in(streams_of[11], part), 12)
    queries = draw_queries(jax.random.fold_in(jax.random.fold_in(streams_of[11], part), 71), part)
    kv_cache = draw_kv_cache(jax.random.fold_in(jax.random.fold_in(streams_of[11], part), 71), part)
    new_kv = scatter_about(part_splits[2], (REQ, 2 * KVH * HD), 1.0, 4.0, ((0, 32),))
    lengths = draw_lengths(jax.random.fold_in(jax.random.fold_in(streams_of[11], part), 71), part)
    residual = draw_residual(jax.random.fold_in(jax.random.fold_in(streams_of[11], part), 71), part)
    w_out = scatter_about(streams_of[5], (HQ * HD, D), 0.1, 0.59765625, ((0, 4),))
    norm_gain = jnp.clip(jax.random.uniform(streams_of[6], (D,), jnp.float32, 0.5, 1.5), 0.5, 1.5)
    expert_ids_keys = jax.random.split(jax.random.fold_in(part_splits[7], 1), REQ // REQ_DEV)
    expert_ids_turns = jax.random.permutation(jax.random.fold_in(part_splits[7], 3), REQ // REQ_DEV)
    expert_ids = jax.vmap(lambda own, number: routed_block(jax.random.fold_in(part_splits[7], 2), own, number, REQ_DEV, EXPERTS, TOPK, MOST, 2))(expert_ids_keys, expert_ids_turns).reshape((REQ, TOPK))
    route_level = with_ends(jax.random.randint(part_splits[8], (REQ, TOPK), 1, 256), jax.random.fold_in(part_splits[8], 1), 1, 255).astype(jnp.int32)
    w_in = scatter_about(streams_of[9], (SHARDS, D, FF), D ** -0.5, 0.125, ((0, 32),))
    w_down = scatter_about(streams_of[10], (SHARDS, FH, D), (FF // 4) ** -0.5, 0.4375, ((0, 32),))
    return {"queries": queries, "kv_cache": kv_cache, "new_kv": new_kv, "lengths": lengths, "residual": residual, "w_out": w_out, "norm_gain": norm_gain, "expert_ids": expert_ids, "route_level": route_level, "w_in": w_in, "w_down": w_down}


def attend_block(operands):
    queries, kv_cache, new_kv, lengths = operands
    req_rows = queries.shape[0]
    group_size = HQ // KVH
    split_at = KVH * HD
    grouped_q = queries.astype(jnp.float32).reshape(req_rows, KVH, group_size, HD)
    key_rows = kv_cache[:, :, :split_at].astype(jnp.float32).reshape(req_rows, CACHE, KVH, HD)
    value_rows = kv_cache[:, :, split_at:].astype(jnp.float32).reshape(req_rows, CACHE, KVH, HD)
    new_key = new_kv[:, :split_at].astype(jnp.float32).reshape(req_rows, KVH, HD)
    new_value = new_kv[:, split_at:].astype(jnp.float32).reshape(req_rows, KVH, HD)
    scaling = 1.0 / math.sqrt(HD)
    scores = jnp.einsum('rgqd,rlgd->rgql', grouped_q, key_rows, precision=lax.Precision.HIGHEST) * scaling
    own_score = jnp.einsum('rgqd,rgd->rgq', grouped_q, new_key, precision=lax.Precision.HIGHEST) * scaling
    visible = (jnp.arange(CACHE)[None, :] < lengths[:, None])[:, None, None, :]
    scores = jnp.where(visible, scores, -jnp.inf)
    peak = jnp.maximum(lax.optimization_barrier(jnp.max(scores, axis=3)), own_score)
    weights = jnp.where(visible, jnp.exp(scores - peak[..., None]), 0.0)
    own_weight = jnp.exp(own_score - peak)
    denominator = lax.optimization_barrier(jnp.sum(weights, axis=3)) + own_weight
    probability = lax.optimization_barrier((weights / denominator[..., None]).astype(jnp.bfloat16)).astype(jnp.float32)
    own_prob = lax.optimization_barrier((own_weight / denominator).astype(jnp.bfloat16)).astype(jnp.float32)
    mixed = jnp.einsum('rgql,rlgd->rgqd', probability, value_rows, precision=lax.Precision.HIGHEST)
    mixed = mixed + own_prob[..., None] * new_value[:, :, None, :]
    return mixed.reshape(req_rows, HQ * HD).astype(jnp.bfloat16)

def reference(queries, kv_cache, new_kv, lengths, residual, w_out, norm_gain, expert_ids, route_level, w_in, w_down):
    blocks = REQ // REQ_DEV
    attended = lax.map(attend_block, (queries.reshape(blocks, REQ_DEV, HQ * HD), kv_cache.reshape(blocks, REQ_DEV, CACHE, 2 * KVH * HD), new_kv.reshape(blocks, REQ_DEV, 2 * KVH * HD), lengths.reshape(blocks, REQ_DEV)))
    attended = attended.reshape(REQ, HQ * HD)
    stream_f = residual.astype(jnp.float32) + jnp.dot(attended, w_out, preferred_element_type=jnp.float32)
    mean_square = lax.optimization_barrier(jnp.mean(stream_f * stream_f, axis=1, keepdims=True))
    normed = (stream_f * lax.rsqrt(mean_square + 1e-06) * norm_gain[None, :]).astype(jnp.bfloat16)
    shares = route_level.astype(jnp.float32)
    shares = shares / lax.optimization_barrier(jnp.sum(shares, axis=1, keepdims=True))
    rows_max = MOST * SHARDS

    def per_expert(expert_acc, expert):
        matches = expert_ids == expert
        chosen = jnp.any(matches, axis=1)
        weight = lax.optimization_barrier(jnp.sum(jnp.where(matches, shares, 0.0), axis=1))
        ordering = jnp.argsort(jnp.logical_not(chosen).astype(jnp.int32), stable=True)[:rows_max].astype(jnp.int32)
        picked = normed[ordering]
        usable = chosen[ordering]
        accum = jnp.zeros((rows_max, D), jnp.float32)
        for half_index in range(2):
            shard_index = 2 * expert + half_index
            gate_up = jnp.dot(picked, w_in[shard_index], preferred_element_type=jnp.float32)
            hidden = (jax.nn.silu(gate_up[:, :FH]) * gate_up[:, FH:]).astype(jnp.bfloat16)
            accum = accum + jnp.dot(hidden, w_down[shard_index], preferred_element_type=jnp.float32)
        rounded = lax.optimization_barrier(accum.astype(jnp.bfloat16)).astype(jnp.float32)
        weighted = jnp.where(usable[:, None], weight[ordering][:, None] * rounded, 0.0)
        return (expert_acc.at[ordering].add(weighted), None)
    expert_acc, unused = lax.scan(per_expert, jnp.zeros((REQ, D), jnp.float32), jnp.arange(EXPERTS, dtype=jnp.int32))
    return (stream_f.astype(jnp.bfloat16), expert_acc.astype(jnp.bfloat16))
```

```python
import functools
import math

import jax
import jax.numpy as jnp
from jax import lax
from jax.experimental import pallas as pl
from jax.experimental.pallas import tpu as pltpu
from jax.sharding import PartitionSpec as P

HD = 128
LANES = 128
MESH = pl.DeviceIdType.MESH
F32 = jnp.float32
BF16 = jnp.bfloat16


def kernel(
    devs,
    sides,
    lengths_ref,
    queries_ref,
    new_kv_ref,
    residual_ref,
    gain_ref,
    ids_ref,
    level_ref,
    kv_hbm,
    w_out_hbm,
    w_in_hbm,
    w_down_hbm,
    stream_ref,
    sum_ref,
    kv,
    w_out,
    w_in,
    w_down,
    by_head,
    mixed_out,
    mixed_in,
    part_out,
    part_in,
    part_own,
    gathered,
    hidden,
    half_out,
    half_in,
    half_own,
    pair_out,
    pair_in,
    last_out,
    last_in,
    kv_sem,
    weight_sem,
    mixed_send,
    mixed_recv,
    part_send,
    part_recv,
    dev_send,
    dev_recv,
    across_send,
    across_recv,
    sib_send,
    sib_recv,
    half_send,
    half_recv,
    pair_send,
    pair_recv,
    last_send,
    last_recv,
):
    rows, width = residual_ref.shape
    cache = kv_hbm.shape[1]
    heads = queries_ref.shape[1] // HD
    split = new_kv_ref.shape[1] // 2
    kv_heads = split // HD
    group = heads // kv_heads
    side_heads = heads // sides
    pairs = sides // 2
    units = w_down_hbm.shape[1]
    me_d = lax.axis_index("dev")
    me_s = lax.axis_index("side")
    me_p, me_c = me_s // 2, me_s % 2
    sib_s = 2 * me_p + 1 - me_c
    sent = []

    def send(src, dst, send_sem, recv_sem, dev, side):
        copy = pltpu.make_async_remote_copy(
            src_ref=src,
            dst_ref=dst,
            send_sem=send_sem,
            recv_sem=recv_sem,
            device_id={"dev": dev, "side": side},
            device_id_type=MESH,
        )
        copy.start()
        sent.append(copy)

    def arrive(dst, send_sem, recv_sem):
        pltpu.make_async_remote_copy(
            src_ref=dst,
            dst_ref=dst,
            send_sem=send_sem,
            recv_sem=recv_sem,
            device_id={"dev": me_d, "side": sib_s},
            device_id_type=MESH,
        ).wait_recv()

    barrier = pltpu.get_barrier_semaphore()
    for k in range(1, sides):
        pl.semaphore_signal(
            barrier, inc=1, device_id={"side": (me_s + k) % sides}, device_id_type=MESH
        )
    for k in range(1, devs):
        pl.semaphore_signal(
            barrier, inc=1, device_id={"dev": (me_d + k) % devs}, device_id_type=MESH
        )

    kv_copies = []
    for r in range(rows):
        kv_copies.append(pltpu.make_async_copy(kv_hbm.at[r], kv.at[r], kv_sem.at[r]))
        kv_copies[-1].start()
    out_copy = pltpu.make_async_copy(w_out_hbm, w_out, weight_sem.at[0])
    in_copy = pltpu.make_async_copy(w_in_hbm.at[0], w_in, weight_sem.at[1])
    down_copy = pltpu.make_async_copy(w_down_hbm.at[0], w_down, weight_sem.at[2])
    out_copy.start()
    in_copy.start()
    down_copy.start()

    for h in range(heads):
        by_head[pl.ds(h, rows, stride=heads), :] = queries_ref[:, h * HD : (h + 1) * HD].astype(F32)
    new_key = new_kv_ref[:, :split].astype(F32)
    new_value = new_kv_ref[:, split:].astype(F32)
    scaling = 1.0 / math.sqrt(HD)
    head_group = lax.broadcasted_iota(jnp.int32, (heads, split), 0) // group
    lane_group = lax.broadcasted_iota(jnp.int32, (heads, split), 1) // HD
    own_lanes = head_group == lane_group
    position = lax.broadcasted_iota(jnp.int32, (heads, cache), 1)
    for r in range(rows):
        kv_copies[r].wait()
        query = by_head[r * heads : (r + 1) * heads, :]
        wide = jnp.where(own_lanes, jnp.concatenate([query] * kv_heads, axis=1), 0.0)
        scores = (
            lax.dot_general(
                wide.astype(BF16),
                kv[r, :, :split],
                (((1,), (1,)), ((), ())),
                preferred_element_type=F32,
            )
            * scaling
        )
        own_score = jnp.sum(wide * new_key[r : r + 1, :], axis=1, keepdims=True) * scaling
        visible = position < lengths_ref[r]
        scores = jnp.where(visible, scores, -jnp.inf)
        peak = jnp.maximum(jnp.max(scores, axis=1, keepdims=True), own_score)
        weights = jnp.exp(scores - peak)
        own_weight = jnp.exp(own_score - peak)
        denominator = jnp.sum(weights, axis=1, keepdims=True) + own_weight
        probability = (weights / denominator).astype(BF16)
        own_prob = (own_weight / denominator).astype(BF16).astype(F32)
        mixed = jnp.dot(probability, kv[r, :, split:], preferred_element_type=F32)
        mixed = jnp.where(own_lanes, mixed + own_prob * new_value[r : r + 1, :], 0.0)
        narrow = mixed[:, :HD]
        for g in range(1, kv_heads):
            narrow = narrow + mixed[:, g * HD : (g + 1) * HD]
        by_head[r * heads : (r + 1) * heads, :] = narrow
    for s in range(sides):
        taken = [
            by_head[pl.ds(s * side_heads + h, rows, stride=heads), :] for h in range(side_heads)
        ]
        mixed_out[s] = jnp.concatenate(taken, axis=1).astype(BF16)

    pl.semaphore_wait(barrier, sides - 1 + devs - 1)
    for k in range(1, sides):
        to = (me_s + k) % sides
        send(
            mixed_out.at[to], mixed_in.at[me_s], mixed_send.at[k - 1], mixed_recv.at[k - 1], me_d, to
        )
    mixed_in[me_s] = mixed_out[me_s]
    ids = ids_ref[...]
    levels = level_ref[...].astype(F32)
    expert_lane = lax.broadcasted_iota(jnp.int32, (rows, LANES), 1)
    spread = jnp.zeros((rows, LANES), F32)
    for k in range(ids.shape[1]):
        spread = spread + jnp.where(ids[:, k : k + 1] == expert_lane, levels[:, k : k + 1], 0.0)
    gathered[me_p, me_d, me_c, :, width:] = spread.astype(BF16)
    out_copy.wait()
    for k in range(1, sides):
        arrive(mixed_in.at[(me_s + sides - k) % sides], mixed_send.at[k - 1], mixed_recv.at[k - 1])
    features = jnp.concatenate([mixed_in[s].astype(F32) for s in range(sides)], axis=0)
    part = jnp.dot(features.astype(BF16), w_out[...], preferred_element_type=F32)
    part = part.reshape(sides, rows, width)
    part_own[...] = part
    part_out[...] = part.astype(BF16)
    for k in range(1, sides):
        to = (me_s + k) % sides
        send(part_out.at[to], part_in.at[k - 1], part_send.at[k - 1], part_recv.at[k - 1], me_d, to)
    stream = residual_ref[...].astype(F32) + part_own[me_s]
    for k in range(1, sides):
        arrive(part_in.at[k - 1], part_send.at[k - 1], part_recv.at[k - 1])
        stream = stream + part_in[k - 1].astype(F32)
    mean_square = jnp.mean(stream * stream, axis=1, keepdims=True)
    normed = stream * lax.rsqrt(mean_square + 1e-06) * gain_ref[...]
    gathered[me_p, me_d, me_c, :, :width] = normed.astype(BF16)

    def share(j, k, block):
        send(block, block, sib_send.at[j, k], sib_recv.at[j, k], me_d, sib_s)

    def across(k, block):
        for j in range(1, pairs):
            to = 2 * ((me_p + j) % pairs) + me_c
            send(block, block, across_send.at[j - 1, k], across_recv.at[j - 1, k], me_d, to)

    mine = gathered.at[me_p, me_d, me_c]
    for k in range(1, devs):
        send(mine, mine, dev_send.at[k - 1], dev_recv.at[k - 1], (me_d + k) % devs, me_s)
    across(0, mine)
    share(0, 0, mine)
    stream_ref[...] = stream.astype(BF16)
    for k in range(1, devs):
        block = gathered.at[me_p, (me_d + devs - k) % devs, me_c]
        arrive(block, dev_send.at[k - 1], dev_recv.at[k - 1])
        across(k, block)
        share(0, k, block)

    def from_sibling(j):
        for k in range(devs):
            block = gathered.at[(me_p + pairs - j) % pairs, (me_d + devs - k) % devs, 1 - me_c]
            arrive(block, sib_send.at[j, k], sib_recv.at[j, k])

    tokens = devs * 2 * rows
    expert = me_d * pairs + me_p
    token_lane = lax.broadcasted_iota(jnp.int32, (tokens, LANES), 1)

    def first_half(j):
        block = gathered[(me_p + pairs - j) % pairs].astype(F32).reshape(tokens, width + LANES)
        gate_up = jnp.dot(block[:, :width].astype(BF16), w_in[...], preferred_element_type=F32)
        gate = gate_up[:, :units]
        hidden[j] = (gate / (1.0 + jnp.exp(-gate)) * gate_up[:, units:]).astype(BF16)

    def second_half(j):
        level = gathered[(me_p + pairs - j) % pairs, :, :, :, width:].astype(F32)
        level = level.reshape(tokens, LANES)
        chosen = jnp.sum(jnp.where(token_lane == expert, level, 0.0), axis=1, keepdims=True)
        weight = chosen / jnp.sum(level, axis=1, keepdims=True)
        out = jnp.dot(hidden[j], w_down[...], preferred_element_type=F32) * weight
        out = out.reshape(devs, 2, rows, width)
        half_own[j] = jnp.where(me_c == 0, out[:, 0], out[:, 1])
        half_out[j] = jnp.where(me_c == 0, out[:, 1], out[:, 0]).astype(BF16)
        send(half_out.at[j], half_in.at[j], half_send.at[j], half_recv.at[j], me_d, sib_s)

    in_copy.wait()
    from_sibling(0)
    first_half(0)
    for j in range(1, pairs):
        for k in range(devs):
            block = gathered.at[(me_p + pairs - j) % pairs, (me_d + devs - k) % devs, me_c]
            arrive(block, across_send.at[j - 1, k], across_recv.at[j - 1, k])
            share(j, k, block)
    down_copy.wait()
    for j in range(1, pairs):
        from_sibling(j)
        first_half(j)
        second_half(j)
    second_half(0)

    for j in range(1, pairs):
        arrive(half_in.at[j], half_send.at[j], half_recv.at[j])
        to = 2 * ((me_p + pairs - j) % pairs) + me_c
        for k in range(1, devs + 1):
            dev = (me_d + k) % devs
            pair_out[j - 1, dev] = (half_own[j, dev] + half_in[j, dev].astype(F32)).astype(BF16)
            send(
                pair_out.at[j - 1, dev],
                pair_in.at[j - 1, dev],
                pair_send.at[j - 1, k - 1],
                pair_recv.at[j - 1, k - 1],
                me_d,
                to,
            )
    arrive(half_in.at[0], half_send.at[0], half_recv.at[0])
    total = None
    for k in range(1, devs + 1):
        dev = (me_d + k) % devs
        total = half_own[0, dev] + half_in[0, dev].astype(F32)
        for j in range(1, pairs):
            arrive(pair_in.at[j - 1, dev], pair_send.at[j - 1, k - 1], pair_recv.at[j - 1, k - 1])
            total = total + pair_in[j - 1, dev].astype(F32)
        if k < devs:
            last_out[k - 1] = total.astype(BF16)
            send(
                last_out.at[k - 1],
                last_in.at[k - 1],
                last_send.at[k - 1],
                last_recv.at[k - 1],
                dev,
                me_s,
            )
    for k in range(1, devs):
        arrive(last_in.at[k - 1], last_send.at[k - 1], last_recv.at[k - 1])
        total = total + last_in[k - 1].astype(F32)
    sum_ref[...] = total.astype(BF16)
    for copy in sent:
        copy.wait_send()


def body(
    queries,
    kv_cache,
    new_kv,
    lengths,
    residual,
    w_out,
    norm_gain,
    expert_ids,
    route_level,
    w_in,
    w_down,
):
    devs, sides = lax.axis_size("dev"), lax.axis_size("side")
    pairs = sides // 2
    rows, width = residual.shape
    heads = queries.shape[1] // HD
    units = w_down.shape[1]
    tokens = devs * 2 * rows
    dma = pltpu.SemaphoreType.DMA
    vmem = pl.BlockSpec(memory_space=pltpu.VMEM)
    hbm = pl.BlockSpec(memory_space=pl.ANY)
    return pl.pallas_call(
        functools.partial(kernel, devs, sides),
        out_shape=(
            jax.ShapeDtypeStruct((rows, width), BF16),
            jax.ShapeDtypeStruct((rows, width), BF16),
        ),
        in_specs=[pl.BlockSpec(memory_space=pltpu.SMEM)] + [vmem] * 6 + [hbm] * 4,
        out_specs=(vmem, vmem),
        scratch_shapes=[
            pltpu.VMEM(kv_cache.shape, BF16),
            pltpu.VMEM(w_out.shape, BF16),
            pltpu.VMEM(w_in.shape[1:], BF16),
            pltpu.VMEM(w_down.shape[1:], BF16),
            pltpu.VMEM((rows * heads, HD), F32),
            pltpu.VMEM((sides, rows, w_out.shape[0]), BF16),
            pltpu.VMEM((sides, rows, w_out.shape[0]), BF16),
            pltpu.VMEM((sides, rows, width), BF16),
            pltpu.VMEM((sides - 1, rows, width), BF16),
            pltpu.VMEM((sides, rows, width), F32),
            pltpu.VMEM((pairs, devs, 2, rows, width + LANES), BF16),
            pltpu.VMEM((pairs, tokens, units), BF16),
            pltpu.VMEM((pairs, devs, rows, width), BF16),
            pltpu.VMEM((pairs, devs, rows, width), BF16),
            pltpu.VMEM((pairs, devs, rows, width), F32),
            pltpu.VMEM((max(1, pairs - 1), devs, rows, width), BF16),
            pltpu.VMEM((max(1, pairs - 1), devs, rows, width), BF16),
            pltpu.VMEM((devs - 1, rows, width), BF16),
            pltpu.VMEM((devs - 1, rows, width), BF16),
            dma((rows,)),
            dma((3,)),
            dma((sides - 1,)),
            dma((sides - 1,)),
            dma((sides - 1,)),
            dma((sides - 1,)),
            dma((devs - 1,)),
            dma((devs - 1,)),
            dma((max(1, pairs - 1), devs)),
            dma((max(1, pairs - 1), devs)),
            dma((pairs, devs)),
            dma((pairs, devs)),
            dma((pairs,)),
            dma((pairs,)),
            dma((max(1, pairs - 1), devs)),
            dma((max(1, pairs - 1), devs)),
            dma((devs - 1,)),
            dma((devs - 1,)),
        ],
        compiler_params=pltpu.CompilerParams(
            collective_id=0, has_side_effects=True, vmem_limit_bytes=56 * 1024 * 1024
        ),
    )(
        lengths,
        queries,
        new_kv,
        residual,
        norm_gain.reshape(1, -1),
        expert_ids,
        route_level,
        kv_cache,
        w_out,
        w_in,
        w_down,
    )


def solution(mesh):
    return jax.shard_map(
        body,
        mesh=mesh,
        in_specs=(
            P(("groups", "dev", "side"), None),
            P(("groups", "dev", "side"), None, None),
            P(("groups", "dev", "side"), None),
            P(("groups", "dev", "side")),
            P(("groups", "dev", "side"), None),
            P("side", None),
            P(),
            P(("groups", "dev", "side"), None),
            P(("groups", "dev", "side"), None),
            P(("dev", "side"), None, None),
            P(("dev", "side"), None, None),
        ),
        out_specs=(P(("groups", "dev", "side"), None), P(("groups", "dev", "side"), None)),
        check_vma=False,
    )
```

```python
import functools
import math

import jax
import jax.numpy as jnp
from jax import lax
from jax.experimental import pallas as pl
from jax.experimental.pallas import tpu as pltpu
from jax.sharding import PartitionSpec as P

HD = 128
LANES = 128
MESH = pl.DeviceIdType.MESH
F32 = jnp.float32
BF16 = jnp.bfloat16


def kernel(
    devs,
    sides,
    lengths_ref,
    queries_hbm,
    new_kv_hbm,
    residual_hbm,
    gain_hbm,
    ids_hbm,
    level_hbm,
    kv_hbm,
    w_out_hbm,
    w_in_hbm,
    w_down_hbm,
    stream_ref,
    sum_ref,
    queries_ref,
    new_kv_ref,
    residual_ref,
    gain_ref,
    ids_ref,
    level_ref,
    kv,
    w_out,
    w_in,
    w_down,
    by_head,
    mixed_out,
    mixed_in,
    part_out,
    part_in,
    part_own,
    gathered,
    hidden,
    half_out,
    half_in,
    half_own,
    pair_out,
    pair_in,
    last_out,
    last_in,
    small_sem,
    kv_sem,
    weight_sem,
    mixed_send,
    mixed_recv,
    part_send,
    part_recv,
    dev_send,
    dev_recv,
    across_send,
    across_recv,
    sib_send,
    sib_recv,
    half_send,
    half_recv,
    pair_send,
    pair_recv,
    last_send,
    last_recv,
):
    rows, width = residual_ref.shape
    cache = kv_hbm.shape[1]
    heads = queries_ref.shape[1] // HD
    split = new_kv_ref.shape[1] // 2
    kv_heads = split // HD
    group = heads // kv_heads
    side_heads = heads // sides
    pairs = sides // 2
    units = w_down_hbm.shape[1]
    me_d = lax.axis_index("dev")
    me_s = lax.axis_index("side")
    me_p, me_c = me_s // 2, me_s % 2
    sib_s = 2 * me_p + 1 - me_c
    sent = []

    def send(src, dst, send_sem, recv_sem, dev, side):
        copy = pltpu.make_async_remote_copy(
            src_ref=src,
            dst_ref=dst,
            send_sem=send_sem,
            recv_sem=recv_sem,
            device_id={"dev": dev, "side": side},
            device_id_type=MESH,
        )
        copy.start()
        sent.append(copy)

    def arrive(dst, send_sem, recv_sem):
        pltpu.make_async_remote_copy(
            src_ref=dst,
            dst_ref=dst,
            send_sem=send_sem,
            recv_sem=recv_sem,
            device_id={"dev": me_d, "side": sib_s},
            device_id_type=MESH,
        ).wait_recv()

    small = (
        (queries_hbm, queries_ref),
        (new_kv_hbm, new_kv_ref),
        (residual_hbm, residual_ref),
        (gain_hbm, gain_ref),
        (ids_hbm, ids_ref),
        (level_hbm, level_ref),
    )
    small_copies = [
        pltpu.make_async_copy(src, dst, small_sem.at[i]) for i, (src, dst) in enumerate(small)
    ]
    kv_copies = [pltpu.make_async_copy(kv_hbm.at[r], kv.at[r], kv_sem.at[r]) for r in range(rows)]
    for copy in small_copies[:2] + kv_copies + small_copies[2:]:
        copy.start()
    out_copy = pltpu.make_async_copy(w_out_hbm, w_out, weight_sem.at[0])
    in_copy = pltpu.make_async_copy(w_in_hbm.at[0], w_in, weight_sem.at[1])
    down_copy = pltpu.make_async_copy(w_down_hbm.at[0], w_down, weight_sem.at[2])
    out_copy.start()
    in_copy.start()
    down_copy.start()

    barrier = pltpu.get_barrier_semaphore()
    for k in range(1, sides):
        pl.semaphore_signal(
            barrier, inc=1, device_id={"side": (me_s + k) % sides}, device_id_type=MESH
        )
    for k in range(1, devs):
        pl.semaphore_signal(
            barrier, inc=1, device_id={"dev": (me_d + k) % devs}, device_id_type=MESH
        )

    small_copies[0].wait()
    small_copies[1].wait()
    for h in range(heads):
        by_head[pl.ds(h, rows, stride=heads), :] = queries_ref[:, h * HD : (h + 1) * HD].astype(F32)
    new_key = new_kv_ref[:, :split].astype(F32)
    new_value = new_kv_ref[:, split:].astype(F32)
    scaling = 1.0 / math.sqrt(HD)
    head_group = lax.broadcasted_iota(jnp.int32, (heads, split), 0) // group
    lane_group = lax.broadcasted_iota(jnp.int32, (heads, split), 1) // HD
    own_lanes = head_group == lane_group
    position = lax.broadcasted_iota(jnp.int32, (heads, cache), 1)
    wide = [
        jnp.where(
            own_lanes,
            jnp.concatenate([by_head[r * heads : (r + 1) * heads, :]] * kv_heads, axis=1),
            0.0,
        )
        for r in range(rows)
    ]
    own_score = [
        jnp.sum(wide[r] * new_key[r : r + 1, :], axis=1, keepdims=True) * scaling
        for r in range(rows)
    ]
    for copy in kv_copies:
        copy.wait()
    scores = [
        lax.dot_general(
            wide[r].astype(BF16),
            kv[r, :, :split],
            (((1,), (1,)), ((), ())),
            preferred_element_type=F32,
        )
        for r in range(rows)
    ]
    scores = [
        jnp.where(position < lengths_ref[r], scores[r] * scaling, -jnp.inf) for r in range(rows)
    ]
    peak = [
        jnp.maximum(jnp.max(scores[r], axis=1, keepdims=True), own_score[r]) for r in range(rows)
    ]
    weights = [jnp.exp(scores[r] - peak[r]) for r in range(rows)]
    own_weight = [jnp.exp(own_score[r] - peak[r]) for r in range(rows)]
    denominator = [
        jnp.sum(weights[r], axis=1, keepdims=True) + own_weight[r] for r in range(rows)
    ]
    probability = [(weights[r] / denominator[r]).astype(BF16) for r in range(rows)]
    own_prob = [(own_weight[r] / denominator[r]).astype(BF16).astype(F32) for r in range(rows)]
    mixed = [
        jnp.dot(probability[r], kv[r, :, split:], preferred_element_type=F32) for r in range(rows)
    ]
    for r in range(rows):
        whole = jnp.where(own_lanes, mixed[r] + own_prob[r] * new_value[r : r + 1, :], 0.0)
        narrow = whole[:, :HD]
        for g in range(1, kv_heads):
            narrow = narrow + whole[:, g * HD : (g + 1) * HD]
        by_head[r * heads : (r + 1) * heads, :] = narrow
    for s in range(sides):
        taken = [
            by_head[pl.ds(s * side_heads + h, rows, stride=heads), :] for h in range(side_heads)
        ]
        mixed_out[s] = jnp.concatenate(taken, axis=1).astype(BF16)

    pl.semaphore_wait(barrier, sides - 1 + devs - 1)
    for k in range(1, sides):
        to = (me_s + k) % sides
        send(
            mixed_out.at[to], mixed_in.at[me_s], mixed_send.at[k - 1], mixed_recv.at[k - 1], me_d, to
        )
    mixed_in[me_s] = mixed_out[me_s]
    for copy in small_copies[2:]:
        copy.wait()
    ids = ids_ref[...]
    levels = level_ref[...].astype(F32)
    expert_lane = lax.broadcasted_iota(jnp.int32, (rows, LANES), 1)
    spread = jnp.zeros((rows, LANES), F32)
    for k in range(ids.shape[1]):
        spread = spread + jnp.where(ids[:, k : k + 1] == expert_lane, levels[:, k : k + 1], 0.0)
    gathered[me_p, me_d, me_c, :, width:] = spread.astype(BF16)
    out_copy.wait()
    for k in range(1, sides):
        arrive(mixed_in.at[(me_s + sides - k) % sides], mixed_send.at[k - 1], mixed_recv.at[k - 1])
    features = jnp.concatenate([mixed_in[s].astype(F32) for s in range(sides)], axis=0)
    part = jnp.dot(features.astype(BF16), w_out[...], preferred_element_type=F32)
    part = part.reshape(sides, rows, width)
    part_own[...] = part
    part_out[...] = part.astype(BF16)
    for k in range(1, sides):
        to = (me_s + k) % sides
        send(part_out.at[to], part_in.at[k - 1], part_send.at[k - 1], part_recv.at[k - 1], me_d, to)
    stream = residual_ref[...].astype(F32) + part_own[me_s]
    for k in range(1, sides):
        arrive(part_in.at[k - 1], part_send.at[k - 1], part_recv.at[k - 1])
        stream = stream + part_in[k - 1].astype(F32)
    mean_square = jnp.mean(stream * stream, axis=1, keepdims=True)
    normed = stream * lax.rsqrt(mean_square + 1e-06) * gain_ref[...]
    gathered[me_p, me_d, me_c, :, :width] = normed.astype(BF16)

    def share(j, k, block):
        send(block, block, sib_send.at[j, k], sib_recv.at[j, k], me_d, sib_s)

    def across(k, block):
        for j in range(1, pairs):
            to = 2 * ((me_p + j) % pairs) + me_c
            send(block, block, across_send.at[j - 1, k], across_recv.at[j - 1, k], me_d, to)

    mine = gathered.at[me_p, me_d, me_c]
    for k in range(1, devs):
        send(mine, mine, dev_send.at[k - 1], dev_recv.at[k - 1], (me_d + k) % devs, me_s)
    across(0, mine)
    share(0, 0, mine)
    stream_ref[...] = stream.astype(BF16)
    for k in range(1, devs):
        block = gathered.at[me_p, (me_d + devs - k) % devs, me_c]
        arrive(block, dev_send.at[k - 1], dev_recv.at[k - 1])
        across(k, block)
        share(0, k, block)

    def from_sibling(j):
        for k in range(devs):
            block = gathered.at[(me_p + pairs - j) % pairs, (me_d + devs - k) % devs, 1 - me_c]
            arrive(block, sib_send.at[j, k], sib_recv.at[j, k])

    tokens = devs * 2 * rows
    expert = me_d * pairs + me_p
    token_lane = lax.broadcasted_iota(jnp.int32, (tokens, LANES), 1)

    def first_half(j):
        block = gathered[(me_p + pairs - j) % pairs].astype(F32).reshape(tokens, width + LANES)
        gate_up = jnp.dot(block[:, :width].astype(BF16), w_in[...], preferred_element_type=F32)
        gate = gate_up[:, :units]
        hidden[j] = (gate / (1.0 + jnp.exp(-gate)) * gate_up[:, units:]).astype(BF16)

    def second_half(j):
        level = gathered[(me_p + pairs - j) % pairs, :, :, :, width:].astype(F32)
        level = level.reshape(tokens, LANES)
        chosen = jnp.sum(jnp.where(token_lane == expert, level, 0.0), axis=1, keepdims=True)
        weight = chosen / jnp.sum(level, axis=1, keepdims=True)
        out = jnp.dot(hidden[j], w_down[...], preferred_element_type=F32) * weight
        out = out.reshape(devs, 2, rows, width)
        half_own[j] = jnp.where(me_c == 0, out[:, 0], out[:, 1])
        half_out[j] = jnp.where(me_c == 0, out[:, 1], out[:, 0]).astype(BF16)
        send(half_out.at[j], half_in.at[j], half_send.at[j], half_recv.at[j], me_d, sib_s)

    in_copy.wait()
    from_sibling(0)
    first_half(0)
    for j in range(1, pairs):
        for k in range(devs):
            block = gathered.at[(me_p + pairs - j) % pairs, (me_d + devs - k) % devs, me_c]
            arrive(block, across_send.at[j - 1, k], across_recv.at[j - 1, k])
            share(j, k, block)
    down_copy.wait()
    for j in range(1, pairs):
        from_sibling(j)
        first_half(j)
        second_half(j)
    second_half(0)

    for j in range(1, pairs):
        arrive(half_in.at[j], half_send.at[j], half_recv.at[j])
        to = 2 * ((me_p + pairs - j) % pairs) + me_c
        for k in range(1, devs + 1):
            dev = (me_d + k) % devs
            pair_out[j - 1, dev] = (half_own[j, dev] + half_in[j, dev].astype(F32)).astype(BF16)
            send(
                pair_out.at[j - 1, dev],
                pair_in.at[j - 1, dev],
                pair_send.at[j - 1, k - 1],
                pair_recv.at[j - 1, k - 1],
                me_d,
                to,
            )
    arrive(half_in.at[0], half_send.at[0], half_recv.at[0])
    total = None
    for k in range(1, devs + 1):
        dev = (me_d + k) % devs
        total = half_own[0, dev] + half_in[0, dev].astype(F32)
        for j in range(1, pairs):
            arrive(pair_in.at[j - 1, dev], pair_send.at[j - 1, k - 1], pair_recv.at[j - 1, k - 1])
            total = total + pair_in[j - 1, dev].astype(F32)
        if k < devs:
            last_out[k - 1] = total.astype(BF16)
            send(
                last_out.at[k - 1],
                last_in.at[k - 1],
                last_send.at[k - 1],
                last_recv.at[k - 1],
                dev,
                me_s,
            )
    for k in range(1, devs):
        arrive(last_in.at[k - 1], last_send.at[k - 1], last_recv.at[k - 1])
        total = total + last_in[k - 1].astype(F32)
    sum_ref[...] = total.astype(BF16)
    for copy in sent:
        copy.wait_send()


def hand_out(stream_ref, sum_ref, stream_out, sum_out, sem):
    copies = [
        pltpu.make_async_copy(stream_ref, stream_out, sem.at[0]),
        pltpu.make_async_copy(sum_ref, sum_out, sem.at[1]),
    ]
    for copy in copies:
        copy.start()
    for copy in copies:
        copy.wait()


def body(
    queries,
    kv_cache,
    new_kv,
    lengths,
    residual,
    w_out,
    norm_gain,
    expert_ids,
    route_level,
    w_in,
    w_down,
):
    devs, sides = lax.axis_size("dev"), lax.axis_size("side")
    pairs = sides // 2
    rows, width = residual.shape
    heads = queries.shape[1] // HD
    units = w_down.shape[1]
    tokens = devs * 2 * rows
    dma = pltpu.SemaphoreType.DMA
    vmem = pl.BlockSpec(memory_space=pltpu.VMEM)
    hbm = pl.BlockSpec(memory_space=pl.ANY)
    norm_gain = norm_gain.reshape(1, -1)
    small = (queries, new_kv, residual, norm_gain, expert_ids, route_level)
    results = pl.pallas_call(
        functools.partial(kernel, devs, sides),
        out_shape=(
            jax.ShapeDtypeStruct((rows, width), BF16),
            jax.ShapeDtypeStruct((rows, width), BF16),
        ),
        in_specs=[pl.BlockSpec(memory_space=pltpu.SMEM)] + [hbm] * 10,
        out_specs=(vmem, vmem),
        scratch_shapes=[
            *(pltpu.VMEM(x.shape, x.dtype) for x in small),
            pltpu.VMEM(kv_cache.shape, BF16),
            pltpu.VMEM(w_out.shape, BF16),
            pltpu.VMEM(w_in.shape[1:], BF16),
            pltpu.VMEM(w_down.shape[1:], BF16),
            pltpu.VMEM((rows * heads, HD), F32),
            pltpu.VMEM((sides, rows, w_out.shape[0]), BF16),
            pltpu.VMEM((sides, rows, w_out.shape[0]), BF16),
            pltpu.VMEM((sides, rows, width), BF16),
            pltpu.VMEM((sides - 1, rows, width), BF16),
            pltpu.VMEM((sides, rows, width), F32),
            pltpu.VMEM((pairs, devs, 2, rows, width + LANES), BF16),
            pltpu.VMEM((pairs, tokens, units), BF16),
            pltpu.VMEM((pairs, devs, rows, width), BF16),
            pltpu.VMEM((pairs, devs, rows, width), BF16),
            pltpu.VMEM((pairs, devs, rows, width), F32),
            pltpu.VMEM((max(1, pairs - 1), devs, rows, width), BF16),
            pltpu.VMEM((max(1, pairs - 1), devs, rows, width), BF16),
            pltpu.VMEM((devs - 1, rows, width), BF16),
            pltpu.VMEM((devs - 1, rows, width), BF16),
            dma((len(small),)),
            dma((rows,)),
            dma((3,)),
            dma((sides - 1,)),
            dma((sides - 1,)),
            dma((sides - 1,)),
            dma((sides - 1,)),
            dma((devs - 1,)),
            dma((devs - 1,)),
            dma((max(1, pairs - 1), devs)),
            dma((max(1, pairs - 1), devs)),
            dma((pairs, devs)),
            dma((pairs, devs)),
            dma((pairs,)),
            dma((pairs,)),
            dma((max(1, pairs - 1), devs)),
            dma((max(1, pairs - 1), devs)),
            dma((devs - 1,)),
            dma((devs - 1,)),
        ],
        compiler_params=pltpu.CompilerParams(
            collective_id=0, has_side_effects=True, vmem_limit_bytes=56 * 1024 * 1024
        ),
    )(
        lengths,
        *small,
        kv_cache,
        w_out,
        w_in,
        w_down,
    )
    return pl.pallas_call(
        hand_out,
        out_shape=tuple(jax.ShapeDtypeStruct((rows, width), BF16) for _ in results),
        in_specs=[hbm] * 2,
        out_specs=(hbm, hbm),
        scratch_shapes=[dma((2,))],
        compiler_params=pltpu.CompilerParams(vmem_limit_bytes=56 * 1024 * 1024),
    )(*results)


def solution(mesh):
    return jax.shard_map(
        body,
        mesh=mesh,
        in_specs=(
            P(("groups", "dev", "side"), None),
            P(("groups", "dev", "side"), None, None),
            P(("groups", "dev", "side"), None),
            P(("groups", "dev", "side")),
            P(("groups", "dev", "side"), None),
            P("side", None),
            P(),
            P(("groups", "dev", "side"), None),
            P(("groups", "dev", "side"), None),
            P(("dev", "side"), None, None),
            P(("dev", "side"), None, None),
        ),
        out_specs=(P(("groups", "dev", "side"), None), P(("groups", "dev", "side"), None)),
        check_vma=False,
    )
```

```python
import functools
import math

import jax
import jax.numpy as jnp
from jax import lax
from jax.experimental import pallas as pl
from jax.experimental.pallas import tpu as pltpu
from jax.sharding import PartitionSpec as P

HD = 128
LANES = 128
MESH = pl.DeviceIdType.MESH
F32 = jnp.float32
BF16 = jnp.bfloat16


def kernel(
    devs,
    sides,
    lengths_ref,
    queries_hbm,
    new_kv_hbm,
    residual_hbm,
    gain_hbm,
    ids_hbm,
    level_hbm,
    kv_hbm,
    w_out_hbm,
    w_in_hbm,
    w_down_hbm,
    stream_ref,
    sum_ref,
    queries_ref,
    new_kv_ref,
    residual_ref,
    gain_ref,
    ids_ref,
    level_ref,
    kv,
    w_out,
    w_in,
    w_down,
    by_head,
    mixed_out,
    mixed_in,
    part_out,
    part_in,
    part_own,
    gathered,
    half_out,
    half_in,
    half_own,
    second_out,
    second_in,
    first_out,
    first_in,
    column_out,
    column_in,
    small_sem,
    kv_sem,
    weight_sem,
    mixed_send,
    mixed_recv,
    part_send,
    part_recv,
    column_send,
    column_recv,
    first_send,
    first_recv,
    second_send,
    second_recv,
    sib_send,
    sib_recv,
    half_send,
    half_recv,
    second_back_send,
    second_back_recv,
    first_back_send,
    first_back_recv,
    column_back_send,
    column_back_recv,
):
    rows, width = residual_ref.shape
    cache = kv_hbm.shape[1]
    heads = queries_ref.shape[1] // HD
    split = new_kv_ref.shape[1] // 2
    kv_heads = split // HD
    group = heads // kv_heads
    side_heads = heads // sides
    pairs = sides // 2
    units = w_down_hbm.shape[1]
    me_d = lax.axis_index("dev")
    me_s = lax.axis_index("side")
    me_p, me_c = me_s // 2, me_s % 2
    sib_s = 2 * me_p + 1 - me_c
    near = 2 if devs % 2 == 0 else 1
    columns = devs // near
    me_z, me_y = me_d // near, me_d % near
    flip = me_c if pairs == 2 and near == 2 else 0
    sent = []

    def first_of(p, y):
        return p + flip * (1 - 2 * p), y + (1 - flip) * (1 - 2 * y)

    def second_of(p, y, j):
        return (1 - flip) * ((p + j) % pairs) + flip * p, y + flip * (1 - 2 * y)

    def device(p, z, y):
        return z * near + y, 2 * p + me_c


    def send(src, dst, send_sem, recv_sem, dev, side):
        copy = pltpu.make_async_remote_copy(
            src_ref=src,
            dst_ref=dst,
            send_sem=send_sem,
            recv_sem=recv_sem,
            device_id={"dev": dev, "side": side},
            device_id_type=MESH,
        )
        copy.start()
        sent.append(copy)

    def arrive(dst, send_sem, recv_sem):
        pltpu.make_async_remote_copy(
            src_ref=dst,
            dst_ref=dst,
            send_sem=send_sem,
            recv_sem=recv_sem,
            device_id={"dev": me_d, "side": sib_s},
            device_id_type=MESH,
        ).wait_recv()

    small = (
        (queries_hbm, queries_ref),
        (new_kv_hbm, new_kv_ref),
        (residual_hbm, residual_ref),
        (gain_hbm, gain_ref),
        (ids_hbm, ids_ref),
        (level_hbm, level_ref),
    )
    small_copies = [
        pltpu.make_async_copy(src, dst, small_sem.at[i]) for i, (src, dst) in enumerate(small)
    ]
    kv_copies = [pltpu.make_async_copy(kv_hbm.at[r], kv.at[r], kv_sem.at[r]) for r in range(rows)]
    for copy in small_copies[:2] + kv_copies + small_copies[2:]:
        copy.start()
    out_copy = pltpu.make_async_copy(w_out_hbm, w_out, weight_sem.at[0])
    in_copy = pltpu.make_async_copy(w_in_hbm.at[0], w_in, weight_sem.at[1])
    down_copy = pltpu.make_async_copy(w_down_hbm.at[0], w_down, weight_sem.at[2])
    out_copy.start()
    in_copy.start()
    down_copy.start()

    barrier = pltpu.get_barrier_semaphore()
    for k in range(1, sides):
        pl.semaphore_signal(
            barrier, inc=1, device_id={"side": (me_s + k) % sides}, device_id_type=MESH
        )
    for k in range(1, devs):
        pl.semaphore_signal(
            barrier, inc=1, device_id={"dev": (me_d + k) % devs}, device_id_type=MESH
        )

    small_copies[0].wait()
    small_copies[1].wait()
    for h in range(heads):
        by_head[pl.ds(h, rows, stride=heads), :] = queries_ref[:, h * HD : (h + 1) * HD].astype(F32)
    new_key = new_kv_ref[:, :split].astype(F32)
    new_value = new_kv_ref[:, split:].astype(F32)
    scaling = 1.0 / math.sqrt(HD)
    head_group = lax.broadcasted_iota(jnp.int32, (heads, split), 0) // group
    lane_group = lax.broadcasted_iota(jnp.int32, (heads, split), 1) // HD
    own_lanes = head_group == lane_group
    position = lax.broadcasted_iota(jnp.int32, (heads, cache), 1)
    wide = [
        jnp.where(
            own_lanes,
            jnp.concatenate([by_head[r * heads : (r + 1) * heads, :]] * kv_heads, axis=1),
            0.0,
        )
        for r in range(rows)
    ]
    own_score = [
        jnp.sum(wide[r] * new_key[r : r + 1, :], axis=1, keepdims=True) * scaling
        for r in range(rows)
    ]
    for copy in kv_copies:
        copy.wait()
    scores = [
        lax.dot_general(
            wide[r].astype(BF16),
            kv[r, :, :split],
            (((1,), (1,)), ((), ())),
            preferred_element_type=F32,
        )
        for r in range(rows)
    ]
    scores = [
        jnp.where(position < lengths_ref[r], scores[r] * scaling, -jnp.inf) for r in range(rows)
    ]
    peak = [
        jnp.maximum(jnp.max(scores[r], axis=1, keepdims=True), own_score[r]) for r in range(rows)
    ]
    weights = [jnp.exp(scores[r] - peak[r]) for r in range(rows)]
    own_weight = [jnp.exp(own_score[r] - peak[r]) for r in range(rows)]
    denominator = [
        jnp.sum(weights[r], axis=1, keepdims=True) + own_weight[r] for r in range(rows)
    ]
    probability = [(weights[r] / denominator[r]).astype(BF16) for r in range(rows)]
    own_prob = [(own_weight[r] / denominator[r]).astype(BF16).astype(F32) for r in range(rows)]
    mixed = [
        jnp.dot(probability[r], kv[r, :, split:], preferred_element_type=F32) for r in range(rows)
    ]
    for r in range(rows):
        whole = jnp.where(own_lanes, mixed[r] + own_prob[r] * new_value[r : r + 1, :], 0.0)
        narrow = whole[:, :HD]
        for g in range(1, kv_heads):
            narrow = narrow + whole[:, g * HD : (g + 1) * HD]
        by_head[r * heads : (r + 1) * heads, :] = narrow
    for s in range(sides):
        taken = [
            by_head[pl.ds(s * side_heads + h, rows, stride=heads), :] for h in range(side_heads)
        ]
        mixed_out[s] = jnp.concatenate(taken, axis=1).astype(BF16)

    pl.semaphore_wait(barrier, sides - 1 + devs - 1)
    for k in range(1, sides):
        to = (me_s + k) % sides
        send(
            mixed_out.at[to], mixed_in.at[me_s], mixed_send.at[k - 1], mixed_recv.at[k - 1], me_d, to
        )
    mixed_in[me_s] = mixed_out[me_s]
    for copy in small_copies[2:]:
        copy.wait()
    ids = ids_ref[...]
    levels = level_ref[...].astype(F32)
    expert_lane = lax.broadcasted_iota(jnp.int32, (rows, LANES), 1)
    spread = jnp.zeros((rows, LANES), F32)
    for k in range(ids.shape[1]):
        spread = spread + jnp.where(ids[:, k : k + 1] == expert_lane, levels[:, k : k + 1], 0.0)
    gathered[me_p, me_z, me_y, me_c, :, width:] = spread.astype(BF16)
    out_copy.wait()
    for k in range(1, sides):
        arrive(mixed_in.at[(me_s + sides - k) % sides], mixed_send.at[k - 1], mixed_recv.at[k - 1])
    features = jnp.concatenate([mixed_in[s].astype(F32) for s in range(sides)], axis=0)
    part = jnp.dot(features.astype(BF16), w_out[...], preferred_element_type=F32)
    part = part.reshape(sides, rows, width)
    part_own[...] = part
    part_out[...] = part.astype(BF16)
    for k in range(1, sides):
        to = (me_s + k) % sides
        send(part_out.at[to], part_in.at[k - 1], part_send.at[k - 1], part_recv.at[k - 1], me_d, to)
    stream = residual_ref[...].astype(F32) + part_own[me_s]
    for k in range(1, sides):
        arrive(part_in.at[k - 1], part_send.at[k - 1], part_recv.at[k - 1])
        stream = stream + part_in[k - 1].astype(F32)
    mean_square = jnp.mean(stream * stream, axis=1, keepdims=True)
    normed = stream * lax.rsqrt(mean_square + 1e-06) * gain_ref[...]
    gathered[me_p, me_z, me_y, me_c, :, :width] = normed.astype(BF16)

    def spread_out(k, slot, p, y):
        block = gathered.at[p, (me_z + columns - k) % columns, y, me_c]
        if slot == 0:
            jp, jy = 0, 0
            if near == 2:
                dev, side = device(*before(first_of(me_p, me_y)))
                send(block, block, first_send.at[k], first_recv.at[k], dev, side)
        else:
            jp, jy = flip, 1 - flip
        for j in range(1, pairs):
            dev, side = device(*before(second_of(me_p, me_y, j)))
            sems = second_send.at[j - 1, k, slot], second_recv.at[j - 1, k, slot]
            send(block, block, *sems, dev, side)
        send(block, block, sib_send.at[jp, k, jy], sib_recv.at[jp, k, jy], me_d, sib_s)

    def before(py):
        return py[0], me_z, py[1]

    mine = gathered.at[me_p, me_z, me_y, me_c]
    for k in range(1, columns):
        dev, side = device(me_p, (me_z + k) % columns, me_y)
        send(mine, mine, column_send.at[k - 1], column_recv.at[k - 1], dev, side)
    spread_out(0, 0, me_p, me_y)
    stream_ref[...] = stream.astype(BF16)
    first_p, first_y = first_of(me_p, me_y)

    def take_first(k):
        if near == 2:
            block = gathered.at[first_p, (me_z + columns - k) % columns, first_y, me_c]
            arrive(block, first_send.at[k], first_recv.at[k])
            spread_out(k, 1, first_p, first_y)

    for k in range(1, columns):
        block = gathered.at[me_p, (me_z + columns - k) % columns, me_y, me_c]
        arrive(block, column_send.at[k - 1], column_recv.at[k - 1])
        spread_out(k, 0, me_p, me_y)
        take_first(k - 1)
    take_first(columns - 1)
    for k in range(columns):
        for j in range(1, pairs):
            from_p, from_y = second_of(me_p, me_y, pairs - j)
            for slot in range(near):
                if slot == 1:
                    from_p, from_y = first_of(from_p, from_y)
                block = gathered.at[from_p, (me_z + columns - k) % columns, from_y, me_c]
                arrive(block, second_send.at[j - 1, k, slot], second_recv.at[j - 1, k, slot])
                jp = (1 - flip) * j + flip * slot
                jy = (1 - flip) * slot + flip
                send(block, block, sib_send.at[jp, k, jy], sib_recv.at[jp, k, jy], me_d, sib_s)
    for k in range(columns):
        for jp in range(pairs):
            for jy in range(near):
                block = gathered.at[
                    (me_p + pairs - jp) % pairs,
                    (me_z + columns - k) % columns,
                    (me_y + jy) % near,
                    1 - me_c,
                ]
                arrive(block, sib_send.at[jp, k, jy], sib_recv.at[jp, k, jy])

    in_copy.wait()
    tokens = pairs * devs * 2 * rows
    expert = me_d * pairs + me_p
    token_lane = lax.broadcasted_iota(jnp.int32, (tokens, LANES), 1)
    block = gathered[:, :, :, :, :, :width].astype(F32).reshape(tokens, width).astype(BF16)
    gate_up = jnp.dot(block, w_in[...], preferred_element_type=F32)
    gate = gate_up[:, :units]
    hidden = (gate / (1.0 + jnp.exp(-gate)) * gate_up[:, units:]).astype(BF16)
    level = gathered[:, :, :, :, :, width:].astype(F32).reshape(tokens, LANES)
    chosen = jnp.sum(jnp.where(token_lane == expert, level, 0.0), axis=1, keepdims=True)
    weight = chosen / jnp.sum(level, axis=1, keepdims=True)
    down_copy.wait()
    half = width // 2
    for h in range(2):
        out = jnp.dot(
            hidden, w_down[:, h * half : (h + 1) * half], preferred_element_type=F32
        )
        out = (out * weight).reshape(pairs, columns, near, 2, rows, half)
        half_own[h] = jnp.where(me_c == 0, out[:, :, :, 0], out[:, :, :, 1])
        half_out[h] = jnp.where(me_c == 0, out[:, :, :, 1], out[:, :, :, 0]).astype(BF16)
        send(half_out.at[h], half_in.at[h], half_send.at[h], half_recv.at[h], me_d, sib_s)

    def both(h, p, z, y):
        return half_own[h, p, z, y] + half_in[h, p, z, y].astype(F32)

    steps = [(h, k % columns) for h in range(2) for k in range(1, columns + 1)]
    for h, k in steps:
        if k == 1 % columns:
            arrive(half_in.at[h], half_send.at[h], half_recv.at[h])
        z = (me_z + k) % columns
        for j in range(1, pairs):
            to_p, to_y = second_of(me_p, me_y, j)
            dev, side = device(to_p, me_z, to_y)
            for slot in range(near):
                if slot == 1:
                    to_p, to_y = first_of(to_p, to_y)
                second_out[h, j - 1, k, slot] = both(h, to_p, z, to_y).astype(BF16)
            send(
                second_out.at[h, j - 1, k],
                second_in.at[h, j - 1, k],
                second_back_send.at[h, j - 1, k],
                second_back_recv.at[h, j - 1, k],
                dev,
                side,
            )

    def to_first(h, k):
        z = (me_z + k) % columns
        for j in range(1, pairs):
            arrive(
                second_in.at[h, j - 1, k],
                second_back_send.at[h, j - 1, k],
                second_back_recv.at[h, j - 1, k],
            )
        if near == 2:
            total = both(h, first_p, z, first_y)
            for j in range(1, pairs):
                total = total + second_in[h, j - 1, k, 1].astype(F32)
            first_out[h, k] = total.astype(BF16)
            dev, side = device(first_p, me_z, first_y)
            sems = first_back_send.at[h, k], first_back_recv.at[h, k]
            send(first_out.at[h, k], first_in.at[h, k], *sems, dev, side)

    totals = []

    def to_column(h, k):
        z = (me_z + k) % columns
        total = both(h, me_p, z, me_y)
        for j in range(1, pairs):
            total = total + second_in[h, j - 1, k, 0].astype(F32)
        if near == 2:
            arrive(first_in.at[h, k], first_back_send.at[h, k], first_back_recv.at[h, k])
            total = total + first_in[h, k].astype(F32)
        if k == 0:
            totals.append(total)
            return
        column_out[h, k - 1] = total.astype(BF16)
        dev, side = device(me_p, z, me_y)
        sems = column_back_send.at[h, k - 1], column_back_recv.at[h, k - 1]
        send(column_out.at[h, k - 1], column_in.at[h, k - 1], *sems, dev, side)

    for i in range(len(steps) + 2):
        if i < len(steps):
            to_first(*steps[i])
        if i >= 2:
            to_column(*steps[i - 2])
    for h in range(2):
        total = totals[h]
        for k in range(1, columns):
            sems = column_back_send.at[h, k - 1], column_back_recv.at[h, k - 1]
            arrive(column_in.at[h, k - 1], *sems)
            total = total + column_in[h, k - 1].astype(F32)
        sum_ref[:, h * half : (h + 1) * half] = total.astype(BF16)
    for copy in sent:
        copy.wait_send()


def body(
    queries,
    kv_cache,
    new_kv,
    lengths,
    residual,
    w_out,
    norm_gain,
    expert_ids,
    route_level,
    w_in,
    w_down,
):
    devs, sides = lax.axis_size("dev"), lax.axis_size("side")
    pairs = sides // 2
    rows, width = residual.shape
    heads = queries.shape[1] // HD
    near = 2 if devs % 2 == 0 else 1
    columns, half = devs // near, width // 2
    dma = pltpu.SemaphoreType.DMA
    vmem = pl.BlockSpec(memory_space=pltpu.VMEM)
    hbm = pl.BlockSpec(memory_space=pl.ANY)
    norm_gain = norm_gain.reshape(1, -1)
    small = (queries, new_kv, residual, norm_gain, expert_ids, route_level)
    results = pl.pallas_call(
        functools.partial(kernel, devs, sides),
        out_shape=(
            pltpu.VMEM((rows, width), BF16),
            pltpu.VMEM((rows, width), BF16),
        ),
        in_specs=[pl.BlockSpec(memory_space=pltpu.SMEM)] + [hbm] * 10,
        out_specs=(vmem, vmem),
        scratch_shapes=[
            *(pltpu.VMEM(x.shape, x.dtype) for x in small),
            pltpu.VMEM(kv_cache.shape, BF16),
            pltpu.VMEM(w_out.shape, BF16),
            pltpu.VMEM(w_in.shape[1:], BF16),
            pltpu.VMEM(w_down.shape[1:], BF16),
            pltpu.VMEM((rows * heads, HD), F32),
            pltpu.VMEM((sides, rows, w_out.shape[0]), BF16),
            pltpu.VMEM((sides, rows, w_out.shape[0]), BF16),
            pltpu.VMEM((sides, rows, width), BF16),
            pltpu.VMEM((sides - 1, rows, width), BF16),
            pltpu.VMEM((sides, rows, width), F32),
            pltpu.VMEM((pairs, columns, near, 2, rows, width + LANES), BF16),
            pltpu.VMEM((2, pairs, columns, near, rows, half), BF16),
            pltpu.VMEM((2, pairs, columns, near, rows, half), BF16),
            pltpu.VMEM((2, pairs, columns, near, rows, half), F32),
            pltpu.VMEM((2, max(1, pairs - 1), columns, near, rows, half), BF16),
            pltpu.VMEM((2, max(1, pairs - 1), columns, near, rows, half), BF16),
            pltpu.VMEM((2, columns, rows, half), BF16),
            pltpu.VMEM((2, columns, rows, half), BF16),
            pltpu.VMEM((2, max(1, columns - 1), rows, half), BF16),
            pltpu.VMEM((2, max(1, columns - 1), rows, half), BF16),
            dma((len(small),)),
            dma((rows,)),
            dma((3,)),
            *[dma((sides - 1,))] * 4,
            *[dma((max(1, columns - 1),))] * 2,
            *[dma((columns,))] * 2,
            *[dma((max(1, pairs - 1), columns, near))] * 2,
            *[dma((pairs, columns, near))] * 2,
            *[dma((2,))] * 2,
            *[dma((2, max(1, pairs - 1), columns))] * 2,
            *[dma((2, columns))] * 2,
            *[dma((2, max(1, columns - 1)))] * 2,
        ],
        compiler_params=pltpu.CompilerParams(
            collective_id=0, has_side_effects=True, vmem_limit_bytes=56 * 1024 * 1024
        ),
    )(
        lengths,
        *small,
        kv_cache,
        w_out,
        w_in,
        w_down,
    )
    return results


def solution(mesh):
    return jax.shard_map(
        body,
        mesh=mesh,
        in_specs=(
            P(("groups", "dev", "side"), None),
            P(("groups", "dev", "side"), None, None),
            P(("groups", "dev", "side"), None),
            P(("groups", "dev", "side")),
            P(("groups", "dev", "side"), None),
            P("side", None),
            P(),
            P(("groups", "dev", "side"), None),
            P(("groups", "dev", "side"), None),
            P(("dev", "side"), None, None),
            P(("dev", "side"), None, None),
        ),
        out_specs=(P(("groups", "dev", "side"), None), P(("groups", "dev", "side"), None)),
        check_vma=False,
    )
```

```python
import functools
import math

import jax
import jax.numpy as jnp
from jax import lax
from jax.experimental import pallas as pl
from jax.experimental.pallas import tpu as pltpu
from jax.sharding import PartitionSpec as P

HD = 128
LANES = 128
MESH = pl.DeviceIdType.MESH
F32 = jnp.float32
BF16 = jnp.bfloat16


def kernel(
    devs,
    sides,
    lengths_ref,
    queries_hbm,
    new_kv_hbm,
    residual_hbm,
    gain_hbm,
    ids_hbm,
    level_hbm,
    kv_hbm,
    w_out_hbm,
    w_in_hbm,
    w_down_hbm,
    stream_ref,
    sum_ref,
    queries_ref,
    new_kv_ref,
    residual_ref,
    gain_ref,
    ids_ref,
    level_ref,
    kv,
    w_out,
    w_in,
    w_down,
    by_head,
    mixed_out,
    mixed_in,
    part_out,
    part_in,
    part_own,
    gathered,
    half_out,
    half_in,
    half_own,
    pair_out,
    pair_in,
    last_out,
    last_in,
    small_sem,
    kv_sem,
    weight_sem,
    mixed_send,
    mixed_recv,
    part_send,
    part_recv,
    dev_send,
    dev_recv,
    across_send,
    across_recv,
    sib_send,
    sib_recv,
    half_send,
    half_recv,
    pair_send,
    pair_recv,
    last_send,
    last_recv,
):
    rows, width = residual_ref.shape
    cache = kv_hbm.shape[1]
    heads = queries_ref.shape[1] // HD
    split = new_kv_ref.shape[1] // 2
    kv_heads = split // HD
    group = heads // kv_heads
    side_heads = heads // sides
    pairs = sides // 2
    units = w_down_hbm.shape[1]
    me_d = lax.axis_index("dev")
    me_s = lax.axis_index("side")
    me_p, me_c = me_s // 2, me_s % 2
    sib_s = 2 * me_p + 1 - me_c
    sent = []

    def send(src, dst, send_sem, recv_sem, dev, side):
        copy = pltpu.make_async_remote_copy(
            src_ref=src,
            dst_ref=dst,
            send_sem=send_sem,
            recv_sem=recv_sem,
            device_id={"dev": dev, "side": side},
            device_id_type=MESH,
        )
        copy.start()
        sent.append(copy)

    def arrive(dst, send_sem, recv_sem):
        pltpu.make_async_remote_copy(
            src_ref=dst,
            dst_ref=dst,
            send_sem=send_sem,
            recv_sem=recv_sem,
            device_id={"dev": me_d, "side": sib_s},
            device_id_type=MESH,
        ).wait_recv()

    small = (
        (queries_hbm, queries_ref),
        (new_kv_hbm, new_kv_ref),
        (residual_hbm, residual_ref),
        (gain_hbm, gain_ref),
        (ids_hbm, ids_ref),
        (level_hbm, level_ref),
    )
    small_copies = [
        pltpu.make_async_copy(src, dst, small_sem.at[i]) for i, (src, dst) in enumerate(small)
    ]
    kv_copies = [pltpu.make_async_copy(kv_hbm.at[r], kv.at[r], kv_sem.at[r]) for r in range(rows)]
    for copy in small_copies[:2] + kv_copies + small_copies[2:]:
        copy.start()
    out_copy = pltpu.make_async_copy(w_out_hbm, w_out, weight_sem.at[0])
    in_copy = pltpu.make_async_copy(w_in_hbm.at[0], w_in, weight_sem.at[1])
    down_copy = pltpu.make_async_copy(w_down_hbm.at[0], w_down, weight_sem.at[2])
    out_copy.start()
    in_copy.start()
    down_copy.start()

    barrier = pltpu.get_barrier_semaphore()
    for k in range(1, sides):
        pl.semaphore_signal(
            barrier, inc=1, device_id={"side": (me_s + k) % sides}, device_id_type=MESH
        )
    for k in range(1, devs):
        pl.semaphore_signal(
            barrier, inc=1, device_id={"dev": (me_d + k) % devs}, device_id_type=MESH
        )

    small_copies[0].wait()
    small_copies[1].wait()
    for h in range(heads):
        by_head[pl.ds(h, rows, stride=heads), :] = queries_ref[:, h * HD : (h + 1) * HD].astype(F32)
    new_key = new_kv_ref[:, :split].astype(F32)
    new_value = new_kv_ref[:, split:].astype(F32)
    scaling = 1.0 / math.sqrt(HD)
    head_group = lax.broadcasted_iota(jnp.int32, (heads, split), 0) // group
    lane_group = lax.broadcasted_iota(jnp.int32, (heads, split), 1) // HD
    own_lanes = head_group == lane_group
    position = lax.broadcasted_iota(jnp.int32, (heads, cache), 1)
    wide = [
        jnp.where(
            own_lanes,
            jnp.concatenate([by_head[r * heads : (r + 1) * heads, :]] * kv_heads, axis=1),
            0.0,
        )
        for r in range(rows)
    ]
    own_score = [
        jnp.sum(wide[r] * new_key[r : r + 1, :], axis=1, keepdims=True) * scaling
        for r in range(rows)
    ]
    for copy in kv_copies:
        copy.wait()
    scores = [
        lax.dot_general(
            wide[r].astype(BF16),
            kv[r, :, :split],
            (((1,), (1,)), ((), ())),
            preferred_element_type=F32,
        )
        for r in range(rows)
    ]
    scores = [
        jnp.where(position < lengths_ref[r], scores[r] * scaling, -jnp.inf) for r in range(rows)
    ]
    peak = [
        jnp.maximum(jnp.max(scores[r], axis=1, keepdims=True), own_score[r]) for r in range(rows)
    ]
    weights = [jnp.exp(scores[r] - peak[r]) for r in range(rows)]
    own_weight = [jnp.exp(own_score[r] - peak[r]) for r in range(rows)]
    denominator = [
        jnp.sum(weights[r], axis=1, keepdims=True) + own_weight[r] for r in range(rows)
    ]
    probability = [(weights[r] / denominator[r]).astype(BF16) for r in range(rows)]
    own_prob = [(own_weight[r] / denominator[r]).astype(BF16).astype(F32) for r in range(rows)]
    mixed = [
        jnp.dot(probability[r], kv[r, :, split:], preferred_element_type=F32) for r in range(rows)
    ]
    for r in range(rows):
        whole = jnp.where(own_lanes, mixed[r] + own_prob[r] * new_value[r : r + 1, :], 0.0)
        narrow = whole[:, :HD]
        for g in range(1, kv_heads):
            narrow = narrow + whole[:, g * HD : (g + 1) * HD]
        by_head[r * heads : (r + 1) * heads, :] = narrow
    for s in range(sides):
        taken = [
            by_head[pl.ds(s * side_heads + h, rows, stride=heads), :] for h in range(side_heads)
        ]
        mixed_out[s] = jnp.concatenate(taken, axis=1).astype(BF16)

    pl.semaphore_wait(barrier, sides - 1 + devs - 1)
    for k in range(1, sides):
        to = (me_s + k) % sides
        send(
            mixed_out.at[to], mixed_in.at[me_s], mixed_send.at[k - 1], mixed_recv.at[k - 1], me_d, to
        )
    mixed_in[me_s] = mixed_out[me_s]
    for copy in small_copies[2:]:
        copy.wait()
    ids = ids_ref[...]
    levels = level_ref[...].astype(F32)
    expert_lane = lax.broadcasted_iota(jnp.int32, (rows, LANES), 1)
    spread = jnp.zeros((rows, LANES), F32)
    for k in range(ids.shape[1]):
        spread = spread + jnp.where(ids[:, k : k + 1] == expert_lane, levels[:, k : k + 1], 0.0)
    gathered[0, 0, me_c, :, width:] = spread.astype(BF16)
    out_copy.wait()
    for k in range(1, sides):
        arrive(mixed_in.at[(me_s + sides - k) % sides], mixed_send.at[k - 1], mixed_recv.at[k - 1])
    features = jnp.concatenate([mixed_in[s].astype(F32) for s in range(sides)], axis=0)
    part = jnp.dot(features.astype(BF16), w_out[...], preferred_element_type=F32)
    part = part.reshape(sides, rows, width)
    part_own[...] = part
    part_out[...] = part.astype(BF16)
    for k in range(1, sides):
        to = (me_s + k) % sides
        send(part_out.at[to], part_in.at[k - 1], part_send.at[k - 1], part_recv.at[k - 1], me_d, to)
    stream = residual_ref[...].astype(F32) + part_own[me_s]
    for k in range(1, sides):
        arrive(part_in.at[k - 1], part_send.at[k - 1], part_recv.at[k - 1])
        stream = stream + part_in[k - 1].astype(F32)
    mean_square = jnp.mean(stream * stream, axis=1, keepdims=True)
    normed = stream * lax.rsqrt(mean_square + 1e-06) * gain_ref[...]
    gathered[0, 0, me_c, :, :width] = normed.astype(BF16)

    def share(k, j):
        block = gathered.at[k, j, me_c]
        send(block, block, sib_send.at[k, j], sib_recv.at[k, j], me_d, sib_s)

    def across(k):
        for j in range(1, pairs):
            to = 2 * ((me_p + j) % pairs) + me_c
            sems = across_send.at[k, j - 1], across_recv.at[k, j - 1]
            send(gathered.at[k, 0, me_c], gathered.at[k, j, me_c], *sems, me_d, to)

    def from_across(k):
        for j in range(1, pairs):
            arrive(gathered.at[k, j, me_c], across_send.at[k, j - 1], across_recv.at[k, j - 1])
            share(k, j)

    for k in range(1, devs):
        sems = dev_send.at[k - 1], dev_recv.at[k - 1]
        dev = (me_d + k) % devs
        send(gathered.at[0, 0, me_c], gathered.at[k, 0, me_c], *sems, dev, me_s)
    across(0)
    share(0, 0)
    stream_ref[...] = stream.astype(BF16)
    lag = 2
    for k in range(1, devs):
        arrive(gathered.at[k, 0, me_c], dev_send.at[k - 1], dev_recv.at[k - 1])
        across(k)
        share(k, 0)
        if k >= lag:
            from_across(k - lag)

    expert = me_d * pairs + me_p
    ranges = [r for r in ((0, devs // 2), (devs // 2, devs)) if r[0] < r[1]]

    def first_half(first, last):
        for k in range(first, last):
            for j in range(pairs):
                arrive(gathered.at[k, j, 1 - me_c], sib_send.at[k, j], sib_recv.at[k, j])
        tokens = (last - first) * pairs * 2 * rows
        block = gathered[first:last].astype(F32).reshape(tokens, width + LANES)
        level = block[:, width:]
        token_lane = lax.broadcasted_iota(jnp.int32, (tokens, LANES), 1)
        chosen = jnp.sum(jnp.where(token_lane == expert, level, 0.0), axis=1, keepdims=True)
        weight = chosen / jnp.sum(level, axis=1, keepdims=True)
        gate_up = jnp.dot(block[:, :width].astype(BF16), w_in[...], preferred_element_type=F32)
        gate = gate_up[:, :units]
        return (gate / (1.0 + jnp.exp(-gate)) * gate_up[:, units:]).astype(BF16), weight

    def second_half(i, first, last, hidden, weight):
        out = jnp.dot(hidden, w_down[...], preferred_element_type=F32) * weight
        out = out.reshape(last - first, pairs, 2, rows, width)
        half_own[first:last] = jnp.where(me_c == 0, out[:, :, 0], out[:, :, 1])
        half_out[first:last] = jnp.where(me_c == 0, out[:, :, 1], out[:, :, 0]).astype(BF16)
        sems = half_send.at[i], half_recv.at[i]
        send(half_out.at[first:last], half_in.at[first:last], *sems, me_d, sib_s)

    def back_across(i, first, last):
        arrive(half_in.at[first:last], half_send.at[i], half_recv.at[i])
        for k in order(first, last):
            for j in range(1, pairs):
                to = 2 * ((me_p + pairs - j) % pairs) + me_c
                pair_out[k, j - 1] = (half_own[k, j] + half_in[k, j].astype(F32)).astype(BF16)
                sems = pair_send.at[k, j - 1], pair_recv.at[k, j - 1]
                send(pair_out.at[k, j - 1], pair_in.at[k, j - 1], *sems, me_d, to)

    def order(first, last):
        return [k for k in range(first, last) if k > 0] + ([0] if first == 0 else [])

    kept = []

    def back_along(first, last):
        for k in order(first, last):
            total = half_own[k, 0] + half_in[k, 0].astype(F32)
            for j in range(1, pairs):
                arrive(pair_in.at[k, j - 1], pair_send.at[k, j - 1], pair_recv.at[k, j - 1])
                total = total + pair_in[k, j - 1].astype(F32)
            if k == 0:
                kept.append(total)
                continue
            last_out[k - 1] = total.astype(BF16)
            sems = last_send.at[k - 1], last_recv.at[k - 1]
            dev = (me_d + devs - k) % devs
            send(last_out.at[k - 1], last_in.at[k - 1], *sems, dev, me_s)

    in_copy.wait()
    early = first_half(*ranges[0]) if len(ranges) > 1 else None
    for k in range(max(0, devs - lag), devs):
        from_across(k)
    down_copy.wait()
    if early is not None:
        second_half(0, *ranges[0], *early)
    late = first_half(*ranges[-1])
    if early is not None:
        back_across(0, *ranges[0])
    second_half(len(ranges) - 1, *ranges[-1], *late)
    if early is not None:
        back_along(*ranges[0])
    back_across(len(ranges) - 1, *ranges[-1])
    back_along(*ranges[-1])
    total = kept[0]
    for k in range(1, devs):
        arrive(last_in.at[k - 1], last_send.at[k - 1], last_recv.at[k - 1])
        total = total + last_in[k - 1].astype(F32)
    sum_ref[...] = total.astype(BF16)
    for copy in sent:
        copy.wait_send()


def body(
    queries,
    kv_cache,
    new_kv,
    lengths,
    residual,
    w_out,
    norm_gain,
    expert_ids,
    route_level,
    w_in,
    w_down,
):
    devs, sides = lax.axis_size("dev"), lax.axis_size("side")
    pairs = sides // 2
    rows, width = residual.shape
    heads = queries.shape[1] // HD
    dma = pltpu.SemaphoreType.DMA
    vmem = pl.BlockSpec(memory_space=pltpu.VMEM)
    hbm = pl.BlockSpec(memory_space=pl.ANY)
    norm_gain = norm_gain.reshape(1, -1)
    small = (queries, new_kv, residual, norm_gain, expert_ids, route_level)
    return pl.pallas_call(
        functools.partial(kernel, devs, sides),
        out_shape=(
            pltpu.VMEM((rows, width), BF16),
            pltpu.VMEM((rows, width), BF16),
        ),
        in_specs=[pl.BlockSpec(memory_space=pltpu.SMEM)] + [hbm] * 10,
        out_specs=(vmem, vmem),
        scratch_shapes=[
            *(pltpu.VMEM(x.shape, x.dtype) for x in small),
            pltpu.VMEM(kv_cache.shape, BF16),
            pltpu.VMEM(w_out.shape, BF16),
            pltpu.VMEM(w_in.shape[1:], BF16),
            pltpu.VMEM(w_down.shape[1:], BF16),
            pltpu.VMEM((rows * heads, HD), F32),
            pltpu.VMEM((sides, rows, w_out.shape[0]), BF16),
            pltpu.VMEM((sides, rows, w_out.shape[0]), BF16),
            pltpu.VMEM((sides, rows, width), BF16),
            pltpu.VMEM((sides - 1, rows, width), BF16),
            pltpu.VMEM((sides, rows, width), F32),
            pltpu.VMEM((devs, pairs, 2, rows, width + LANES), BF16),
            pltpu.VMEM((devs, pairs, rows, width), BF16),
            pltpu.VMEM((devs, pairs, rows, width), BF16),
            pltpu.VMEM((devs, pairs, rows, width), F32),
            pltpu.VMEM((devs, max(1, pairs - 1), rows, width), BF16),
            pltpu.VMEM((devs, max(1, pairs - 1), rows, width), BF16),
            pltpu.VMEM((devs - 1, rows, width), BF16),
            pltpu.VMEM((devs - 1, rows, width), BF16),
            dma((len(small),)),
            dma((rows,)),
            dma((3,)),
            *[dma((sides - 1,))] * 4,
            *[dma((devs - 1,))] * 2,
            *[dma((devs, max(1, pairs - 1)))] * 2,
            *[dma((devs, pairs))] * 2,
            *[dma((2,))] * 2,
            *[dma((devs, max(1, pairs - 1)))] * 2,
            *[dma((devs - 1,))] * 2,
        ],
        compiler_params=pltpu.CompilerParams(
            collective_id=0, has_side_effects=True, vmem_limit_bytes=56 * 1024 * 1024
        ),
    )(
        lengths,
        *small,
        kv_cache,
        w_out,
        w_in,
        w_down,
    )


def solution(mesh):
    return jax.shard_map(
        body,
        mesh=mesh,
        in_specs=(
            P(("groups", "dev", "side"), None),
            P(("groups", "dev", "side"), None, None),
            P(("groups", "dev", "side"), None),
            P(("groups", "dev", "side")),
            P(("groups", "dev", "side"), None),
            P("side", None),
            P(),
            P(("groups", "dev", "side"), None),
            P(("groups", "dev", "side"), None),
            P(("dev", "side"), None, None),
            P(("dev", "side"), None, None),
        ),
        out_specs=(P(("groups", "dev", "side"), None), P(("groups", "dev", "side"), None)),
        check_vma=False,
    )
```

```python
import functools
import math

import jax
import jax.numpy as jnp
from jax import lax
from jax.experimental import pallas as pl
from jax.experimental.pallas import tpu as pltpu
from jax.sharding import PartitionSpec as P

HD = 128
LANES = 128
MESH = pl.DeviceIdType.MESH
F32 = jnp.float32
BF16 = jnp.bfloat16


def kernel(
    devs,
    sides,
    lengths_ref,
    queries_hbm,
    new_kv_hbm,
    residual_hbm,
    gain_hbm,
    ids_hbm,
    level_hbm,
    kv_hbm,
    w_out_hbm,
    w_in_hbm,
    w_down_hbm,
    stream_ref,
    sum_ref,
    queries_ref,
    new_kv_ref,
    residual_ref,
    gain_ref,
    ids_ref,
    level_ref,
    kv,
    w_out,
    w_in,
    w_down,
    by_head,
    mixed_out,
    mixed_in,
    part_out,
    part_in,
    part_own,
    gathered,
    hidden,
    half_out,
    half_in,
    half_own,
    pair_out,
    pair_in,
    last_out,
    last_in,
    small_sem,
    kv_sem,
    weight_sem,
    mixed_send,
    mixed_recv,
    part_send,
    part_recv,
    dev_send,
    dev_recv,
    across_send,
    across_recv,
    sib_send,
    sib_recv,
    half_send,
    half_recv,
    pair_send,
    pair_recv,
    last_send,
    last_recv,
):
    rows, width = residual_ref.shape
    cache = kv_hbm.shape[1]
    heads = queries_ref.shape[1] // HD
    split = new_kv_ref.shape[1] // 2
    kv_heads = split // HD
    group = heads // kv_heads
    side_heads = heads // sides
    pairs = sides // 2
    units = w_down_hbm.shape[1]
    me_d = lax.axis_index("dev")
    me_s = lax.axis_index("side")
    me_p, me_c = me_s // 2, me_s % 2
    sib_s = 2 * me_p + 1 - me_c
    sent = []

    def send(src, dst, send_sem, recv_sem, dev, side):
        copy = pltpu.make_async_remote_copy(
            src_ref=src,
            dst_ref=dst,
            send_sem=send_sem,
            recv_sem=recv_sem,
            device_id={"dev": dev, "side": side},
            device_id_type=MESH,
        )
        copy.start()
        sent.append(copy)

    def arrive(dst, send_sem, recv_sem):
        pltpu.make_async_remote_copy(
            src_ref=dst,
            dst_ref=dst,
            send_sem=send_sem,
            recv_sem=recv_sem,
            device_id={"dev": me_d, "side": sib_s},
            device_id_type=MESH,
        ).wait_recv()

    small = (
        (queries_hbm, queries_ref),
        (new_kv_hbm, new_kv_ref),
        (residual_hbm, residual_ref),
        (gain_hbm, gain_ref),
        (ids_hbm, ids_ref),
        (level_hbm, level_ref),
    )
    small_copies = [
        pltpu.make_async_copy(src, dst, small_sem.at[i]) for i, (src, dst) in enumerate(small)
    ]
    kv_copies = [pltpu.make_async_copy(kv_hbm.at[r], kv.at[r], kv_sem.at[r]) for r in range(rows)]
    for copy in small_copies[:2] + kv_copies + small_copies[2:]:
        copy.start()
    out_copy = pltpu.make_async_copy(w_out_hbm, w_out, weight_sem.at[0])
    in_copy = pltpu.make_async_copy(w_in_hbm.at[0], w_in, weight_sem.at[1])
    down_copy = pltpu.make_async_copy(w_down_hbm.at[0], w_down, weight_sem.at[2])
    out_copy.start()
    in_copy.start()
    down_copy.start()

    barrier = pltpu.get_barrier_semaphore()
    for k in range(1, sides):
        pl.semaphore_signal(
            barrier, inc=1, device_id={"side": (me_s + k) % sides}, device_id_type=MESH
        )
    for k in range(1, devs):
        pl.semaphore_signal(
            barrier, inc=1, device_id={"dev": (me_d + k) % devs}, device_id_type=MESH
        )

    small_copies[0].wait()
    small_copies[1].wait()
    for h in range(heads):
        by_head[pl.ds(h, rows, stride=heads), :] = queries_ref[:, h * HD : (h + 1) * HD].astype(F32)
    new_key = new_kv_ref[:, :split].astype(F32)
    new_value = new_kv_ref[:, split:].astype(F32)
    scaling = 1.0 / math.sqrt(HD)
    head_group = lax.broadcasted_iota(jnp.int32, (heads, split), 0) // group
    lane_group = lax.broadcasted_iota(jnp.int32, (heads, split), 1) // HD
    own_lanes = head_group == lane_group
    position = lax.broadcasted_iota(jnp.int32, (heads, cache), 1)
    wide = [
        jnp.where(
            own_lanes,
            jnp.concatenate([by_head[r * heads : (r + 1) * heads, :]] * kv_heads, axis=1),
            0.0,
        )
        for r in range(rows)
    ]
    own_score = [
        jnp.sum(wide[r] * new_key[r : r + 1, :], axis=1, keepdims=True) * scaling
        for r in range(rows)
    ]
    for copy in kv_copies:
        copy.wait()
    scores = [
        lax.dot_general(
            wide[r].astype(BF16),
            kv[r, :, :split],
            (((1,), (1,)), ((), ())),
            preferred_element_type=F32,
        )
        for r in range(rows)
    ]
    scores = [
        jnp.where(position < lengths_ref[r], scores[r] * scaling, -jnp.inf) for r in range(rows)
    ]
    peak = [
        jnp.maximum(jnp.max(scores[r], axis=1, keepdims=True), own_score[r]) for r in range(rows)
    ]
    weights = [jnp.exp(scores[r] - peak[r]) for r in range(rows)]
    own_weight = [jnp.exp(own_score[r] - peak[r]) for r in range(rows)]
    denominator = [
        jnp.sum(weights[r], axis=1, keepdims=True) + own_weight[r] for r in range(rows)
    ]
    probability = [(weights[r] / denominator[r]).astype(BF16) for r in range(rows)]
    own_prob = [(own_weight[r] / denominator[r]).astype(BF16).astype(F32) for r in range(rows)]
    mixed = [
        jnp.dot(probability[r], kv[r, :, split:], preferred_element_type=F32) for r in range(rows)
    ]
    for r in range(rows):
        whole = jnp.where(own_lanes, mixed[r] + own_prob[r] * new_value[r : r + 1, :], 0.0)
        narrow = whole[:, :HD]
        for g in range(1, kv_heads):
            narrow = narrow + whole[:, g * HD : (g + 1) * HD]
        by_head[r * heads : (r + 1) * heads, :] = narrow
    for s in range(sides):
        taken = [
            by_head[pl.ds(s * side_heads + h, rows, stride=heads), :] for h in range(side_heads)
        ]
        mixed_out[s] = jnp.concatenate(taken, axis=1).astype(BF16)

    pl.semaphore_wait(barrier, sides - 1 + devs - 1)
    for k in range(1, sides):
        to = (me_s + k) % sides
        send(
            mixed_out.at[to], mixed_in.at[me_s], mixed_send.at[k - 1], mixed_recv.at[k - 1], me_d, to
        )
    mixed_in[me_s] = mixed_out[me_s]
    for copy in small_copies[2:]:
        copy.wait()
    ids = ids_ref[...]
    levels = level_ref[...].astype(F32)
    expert_lane = lax.broadcasted_iota(jnp.int32, (rows, LANES), 1)
    spread = jnp.zeros((rows, LANES), F32)
    for k in range(ids.shape[1]):
        spread = spread + jnp.where(ids[:, k : k + 1] == expert_lane, levels[:, k : k + 1], 0.0)
    gathered[me_p, me_d, me_c, :, width:] = spread.astype(BF16)
    out_copy.wait()
    for k in range(1, sides):
        arrive(mixed_in.at[(me_s + sides - k) % sides], mixed_send.at[k - 1], mixed_recv.at[k - 1])
    features = jnp.concatenate([mixed_in[s].astype(F32) for s in range(sides)], axis=0)
    part = jnp.dot(features.astype(BF16), w_out[...], preferred_element_type=F32)
    part = part.reshape(sides, rows, width)
    part_own[...] = part
    part_out[...] = part.astype(BF16)
    for k in range(1, sides):
        to = (me_s + k) % sides
        send(part_out.at[to], part_in.at[k - 1], part_send.at[k - 1], part_recv.at[k - 1], me_d, to)
    stream = residual_ref[...].astype(F32) + part_own[me_s]
    for k in range(1, sides):
        arrive(part_in.at[k - 1], part_send.at[k - 1], part_recv.at[k - 1])
        stream = stream + part_in[k - 1].astype(F32)
    mean_square = jnp.mean(stream * stream, axis=1, keepdims=True)
    normed = stream * lax.rsqrt(mean_square + 1e-06) * gain_ref[...]
    gathered[me_p, me_d, me_c, :, :width] = normed.astype(BF16)

    def share(j, k, block):
        send(block, block, sib_send.at[j, k], sib_recv.at[j, k], me_d, sib_s)

    def across(k, block):
        for j in range(1, pairs):
            to = 2 * ((me_p + j) % pairs) + me_c
            send(block, block, across_send.at[j - 1, k], across_recv.at[j - 1, k], me_d, to)

    mine = gathered.at[me_p, me_d, me_c]
    for k in range(1, devs):
        send(mine, mine, dev_send.at[k - 1], dev_recv.at[k - 1], (me_d + k) % devs, me_s)
    across(0, mine)
    share(0, 0, mine)
    stream_ref[...] = stream.astype(BF16)
    for k in range(1, devs):
        block = gathered.at[me_p, (me_d + devs - k) % devs, me_c]
        arrive(block, dev_send.at[k - 1], dev_recv.at[k - 1])
        across(k, block)
        share(0, k, block)

    def from_sibling(j):
        for k in range(devs):
            block = gathered.at[(me_p + pairs - j) % pairs, (me_d + devs - k) % devs, 1 - me_c]
            arrive(block, sib_send.at[j, k], sib_recv.at[j, k])

    tokens = devs * 2 * rows
    expert = me_d * pairs + me_p
    token_lane = lax.broadcasted_iota(jnp.int32, (tokens, LANES), 1)

    def first_half(j, between=()):
        block = gathered[(me_p + pairs - j) % pairs, :, :, :, :width].astype(F32)
        block = block.reshape(tokens, width).astype(BF16)
        step = units // max(1, len(between))
        for i in range(units // step):
            cols = slice(i * step, (i + 1) * step)
            both = jnp.concatenate(
                [w_in[:, cols], w_in[:, units + i * step : units + (i + 1) * step]], axis=1
            )
            gate_up = jnp.dot(block, both, preferred_element_type=F32)
            gate = gate_up[:, :step]
            hidden[j, :, cols] = (gate / (1.0 + jnp.exp(-gate)) * gate_up[:, step:]).astype(BF16)
            if between:
                from_across(between[i])

    def second_half(j):
        level = gathered[(me_p + pairs - j) % pairs, :, :, :, width:].astype(F32)
        level = level.reshape(tokens, LANES)
        chosen = jnp.sum(jnp.where(token_lane == expert, level, 0.0), axis=1, keepdims=True)
        weight = chosen / jnp.sum(level, axis=1, keepdims=True)
        out = jnp.dot(hidden[j], w_down[...], preferred_element_type=F32) * weight
        out = out.reshape(devs, 2, rows, width)
        half_own[j] = jnp.where(me_c == 0, out[:, 0], out[:, 1])
        half_out[j] = jnp.where(me_c == 0, out[:, 1], out[:, 0]).astype(BF16)
        send(half_out.at[j], half_in.at[j], half_send.at[j], half_recv.at[j], me_d, sib_s)

    def from_across(ks):
        for k in ks:
            for j in range(1, pairs):
                block = gathered.at[(me_p + pairs - j) % pairs, (me_d + devs - k) % devs, me_c]
                arrive(block, across_send.at[j - 1, k], across_recv.at[j - 1, k])
                share(j, k, block)

    in_copy.wait()
    order = list(range(devs))
    cuts = [order[: devs // 2], order[devs // 2 : devs * 3 // 4], order[devs * 3 // 4 : devs - 1]]
    from_across(cuts[0])
    from_sibling(0)
    first_half(0, (cuts[1], cuts[2], order[devs - 1 :]))
    down_copy.wait()
    for j in range(1, pairs):
        from_sibling(j)
        first_half(j)
        second_half(j)
    second_half(0)

    for j in range(1, pairs):
        arrive(half_in.at[j], half_send.at[j], half_recv.at[j])
        to = 2 * ((me_p + pairs - j) % pairs) + me_c
        for k in range(1, devs + 1):
            dev = (me_d + k) % devs
            pair_out[j - 1, dev] = (half_own[j, dev] + half_in[j, dev].astype(F32)).astype(BF16)
            send(
                pair_out.at[j - 1, dev],
                pair_in.at[j - 1, dev],
                pair_send.at[j - 1, k - 1],
                pair_recv.at[j - 1, k - 1],
                me_d,
                to,
            )
    arrive(half_in.at[0], half_send.at[0], half_recv.at[0])
    total = None
    for k in range(1, devs + 1):
        dev = (me_d + k) % devs
        total = half_own[0, dev] + half_in[0, dev].astype(F32)
        for j in range(1, pairs):
            arrive(pair_in.at[j - 1, dev], pair_send.at[j - 1, k - 1], pair_recv.at[j - 1, k - 1])
            total = total + pair_in[j - 1, dev].astype(F32)
        if k < devs:
            last_out[k - 1] = total.astype(BF16)
            send(
                last_out.at[k - 1],
                last_in.at[k - 1],
                last_send.at[k - 1],
                last_recv.at[k - 1],
                dev,
                me_s,
            )
    for k in range(1, devs):
        arrive(last_in.at[k - 1], last_send.at[k - 1], last_recv.at[k - 1])
        total = total + last_in[k - 1].astype(F32)
    sum_ref[...] = total.astype(BF16)
    for copy in sent:
        copy.wait_send()


def body(
    queries,
    kv_cache,
    new_kv,
    lengths,
    residual,
    w_out,
    norm_gain,
    expert_ids,
    route_level,
    w_in,
    w_down,
):
    devs, sides = lax.axis_size("dev"), lax.axis_size("side")
    pairs = sides // 2
    rows, width = residual.shape
    heads = queries.shape[1] // HD
    units = w_down.shape[1]
    tokens = devs * 2 * rows
    dma = pltpu.SemaphoreType.DMA
    vmem = pl.BlockSpec(memory_space=pltpu.VMEM)
    hbm = pl.BlockSpec(memory_space=pl.ANY)
    norm_gain = norm_gain.reshape(1, -1)
    small = (queries, new_kv, residual, norm_gain, expert_ids, route_level)
    return pl.pallas_call(
        functools.partial(kernel, devs, sides),
        out_shape=(
            pltpu.VMEM((rows, width), BF16),
            pltpu.VMEM((rows, width), BF16),
        ),
        in_specs=[pl.BlockSpec(memory_space=pltpu.SMEM)] + [hbm] * 10,
        out_specs=(vmem, vmem),
        scratch_shapes=[
            *(pltpu.VMEM(x.shape, x.dtype) for x in small),
            pltpu.VMEM(kv_cache.shape, BF16),
            pltpu.VMEM(w_out.shape, BF16),
            pltpu.VMEM(w_in.shape[1:], BF16),
            pltpu.VMEM(w_down.shape[1:], BF16),
            pltpu.VMEM((rows * heads, HD), F32),
            pltpu.VMEM((sides, rows, w_out.shape[0]), BF16),
            pltpu.VMEM((sides, rows, w_out.shape[0]), BF16),
            pltpu.VMEM((sides, rows, width), BF16),
            pltpu.VMEM((sides - 1, rows, width), BF16),
            pltpu.VMEM((sides, rows, width), F32),
            pltpu.VMEM((pairs, devs, 2, rows, width + LANES), BF16),
            pltpu.VMEM((pairs, tokens, units), BF16),
            pltpu.VMEM((pairs, devs, rows, width), BF16),
            pltpu.VMEM((pairs, devs, rows, width), BF16),
            pltpu.VMEM((pairs, devs, rows, width), F32),
            pltpu.VMEM((max(1, pairs - 1), devs, rows, width), BF16),
            pltpu.VMEM((max(1, pairs - 1), devs, rows, width), BF16),
            pltpu.VMEM((devs - 1, rows, width), BF16),
            pltpu.VMEM((devs - 1, rows, width), BF16),
            dma((len(small),)),
            dma((rows,)),
            dma((3,)),
            dma((sides - 1,)),
            dma((sides - 1,)),
            dma((sides - 1,)),
            dma((sides - 1,)),
            dma((devs - 1,)),
            dma((devs - 1,)),
            dma((max(1, pairs - 1), devs)),
            dma((max(1, pairs - 1), devs)),
            dma((pairs, devs)),
            dma((pairs, devs)),
            dma((pairs,)),
            dma((pairs,)),
            dma((max(1, pairs - 1), devs)),
            dma((max(1, pairs - 1), devs)),
            dma((devs - 1,)),
            dma((devs - 1,)),
        ],
        compiler_params=pltpu.CompilerParams(
            collective_id=0, has_side_effects=True, vmem_limit_bytes=56 * 1024 * 1024
        ),
    )(
        lengths,
        *small,
        kv_cache,
        w_out,
        w_in,
        w_down,
    )


def solution(mesh):
    return jax.shard_map(
        body,
        mesh=mesh,
        in_specs=(
            P(("groups", "dev", "side"), None),
            P(("groups", "dev", "side"), None, None),
            P(("groups", "dev", "side"), None),
            P(("groups", "dev", "side")),
            P(("groups", "dev", "side"), None),
            P("side", None),
            P(),
            P(("groups", "dev", "side"), None),
            P(("groups", "dev", "side"), None),
            P(("dev", "side"), None, None),
            P(("dev", "side"), None, None),
        ),
        out_specs=(P(("groups", "dev", "side"), None), P(("groups", "dev", "side"), None)),
        check_vma=False,
    )
```

```python
import functools
import math

import jax
import jax.numpy as jnp
from jax import lax
from jax.experimental import pallas as pl
from jax.experimental.pallas import tpu as pltpu
from jax.sharding import PartitionSpec as P

HD = 128
LANES = 128
MESH = pl.DeviceIdType.MESH
F32 = jnp.float32
BF16 = jnp.bfloat16


def kernel(
    devs,
    sides,
    lengths_ref,
    queries_hbm,
    new_kv_hbm,
    residual_hbm,
    gain_hbm,
    ids_hbm,
    level_hbm,
    kv_hbm,
    w_out_hbm,
    w_in_hbm,
    w_down_hbm,
    stream_ref,
    sum_ref,
    queries_ref,
    new_kv_ref,
    residual_ref,
    gain_ref,
    ids_ref,
    level_ref,
    kv,
    w_out,
    w_in,
    w_down,
    by_head,
    mixed_out,
    mixed_in,
    part_out,
    part_in,
    part_own,
    gathered,
    hidden,
    half_out,
    half_in,
    half_own,
    pair_out,
    pair_in,
    last_out,
    last_in,
    small_sem,
    kv_sem,
    weight_sem,
    mixed_send,
    mixed_recv,
    part_send,
    part_recv,
    dev_send,
    dev_recv,
    across_send,
    across_recv,
    sib_send,
    sib_recv,
    half_send,
    half_recv,
    pair_send,
    pair_recv,
    last_send,
    last_recv,
):
    rows, width = residual_ref.shape
    cache = kv_hbm.shape[1]
    heads = queries_ref.shape[1] // HD
    split = new_kv_ref.shape[1] // 2
    kv_heads = split // HD
    group = heads // kv_heads
    side_heads = heads // sides
    pairs = sides // 2
    units = w_down_hbm.shape[1]
    me_d = lax.axis_index("dev")
    me_s = lax.axis_index("side")
    me_p, me_c = me_s // 2, me_s % 2
    sib_s = 2 * me_p + 1 - me_c
    sent = []

    def send(src, dst, send_sem, recv_sem, dev, side):
        copy = pltpu.make_async_remote_copy(
            src_ref=src,
            dst_ref=dst,
            send_sem=send_sem,
            recv_sem=recv_sem,
            device_id={"dev": dev, "side": side},
            device_id_type=MESH,
        )
        copy.start()
        sent.append(copy)

    def arrive(dst, send_sem, recv_sem):
        pltpu.make_async_remote_copy(
            src_ref=dst,
            dst_ref=dst,
            send_sem=send_sem,
            recv_sem=recv_sem,
            device_id={"dev": me_d, "side": sib_s},
            device_id_type=MESH,
        ).wait_recv()

    small = (
        (queries_hbm, queries_ref),
        (new_kv_hbm, new_kv_ref),
        (residual_hbm, residual_ref),
        (gain_hbm, gain_ref),
        (ids_hbm, ids_ref),
        (level_hbm, level_ref),
    )
    small_copies = [
        pltpu.make_async_copy(src, dst, small_sem.at[i]) for i, (src, dst) in enumerate(small)
    ]
    kv_copies = [pltpu.make_async_copy(kv_hbm.at[r], kv.at[r], kv_sem.at[r]) for r in range(rows)]
    for copy in small_copies[:2] + kv_copies + small_copies[2:]:
        copy.start()
    out_copy = pltpu.make_async_copy(w_out_hbm, w_out, weight_sem.at[0])
    in_copy = pltpu.make_async_copy(w_in_hbm.at[0], w_in, weight_sem.at[1])
    down_copy = pltpu.make_async_copy(w_down_hbm.at[0], w_down, weight_sem.at[2])
    out_copy.start()
    in_copy.start()
    down_copy.start()

    barrier = pltpu.get_barrier_semaphore()
    for k in range(1, sides):
        pl.semaphore_signal(
            barrier, inc=1, device_id={"side": (me_s + k) % sides}, device_id_type=MESH
        )
    for k in range(1, devs):
        pl.semaphore_signal(
            barrier, inc=1, device_id={"dev": (me_d + k) % devs}, device_id_type=MESH
        )

    small_copies[0].wait()
    small_copies[1].wait()
    for h in range(heads):
        by_head[pl.ds(h, rows, stride=heads), :] = queries_ref[:, h * HD : (h + 1) * HD].astype(F32)
    new_key = new_kv_ref[:, :split].astype(F32)
    new_value = new_kv_ref[:, split:].astype(F32)
    scaling = 1.0 / math.sqrt(HD)
    head_group = lax.broadcasted_iota(jnp.int32, (heads, split), 0) // group
    lane_group = lax.broadcasted_iota(jnp.int32, (heads, split), 1) // HD
    own_lanes = head_group == lane_group
    position = lax.broadcasted_iota(jnp.int32, (heads, cache), 1)
    wide = [
        jnp.where(
            own_lanes,
            jnp.concatenate([by_head[r * heads : (r + 1) * heads, :]] * kv_heads, axis=1),
            0.0,
        )
        for r in range(rows)
    ]
    own_score = [
        jnp.sum(wide[r] * new_key[r : r + 1, :], axis=1, keepdims=True) * scaling
        for r in range(rows)
    ]
    for copy in kv_copies:
        copy.wait()
    scores = [
        lax.dot_general(
            wide[r].astype(BF16),
            kv[r, :, :split],
            (((1,), (1,)), ((), ())),
            preferred_element_type=F32,
        )
        for r in range(rows)
    ]
    scores = [
        jnp.where(position < lengths_ref[r], scores[r] * scaling, -jnp.inf) for r in range(rows)
    ]
    peak = [
        jnp.maximum(jnp.max(scores[r], axis=1, keepdims=True), own_score[r]) for r in range(rows)
    ]
    weights = [jnp.exp(scores[r] - peak[r]) for r in range(rows)]
    own_weight = [jnp.exp(own_score[r] - peak[r]) for r in range(rows)]
    denominator = [
        jnp.sum(weights[r], axis=1, keepdims=True) + own_weight[r] for r in range(rows)
    ]
    probability = [(weights[r] / denominator[r]).astype(BF16) for r in range(rows)]
    own_prob = [(own_weight[r] / denominator[r]).astype(BF16).astype(F32) for r in range(rows)]
    mixed = [
        jnp.dot(probability[r], kv[r, :, split:], preferred_element_type=F32) for r in range(rows)
    ]
    for r in range(rows):
        whole = jnp.where(own_lanes, mixed[r] + own_prob[r] * new_value[r : r + 1, :], 0.0)
        narrow = whole[:, :HD]
        for g in range(1, kv_heads):
            narrow = narrow + whole[:, g * HD : (g + 1) * HD]
        by_head[r * heads : (r + 1) * heads, :] = narrow
    for s in range(sides):
        taken = [
            by_head[pl.ds(s * side_heads + h, rows, stride=heads), :] for h in range(side_heads)
        ]
        mixed_out[s] = jnp.concatenate(taken, axis=1).astype(BF16)

    pl.semaphore_wait(barrier, sides - 1 + devs - 1)
    for k in range(1, sides):
        to = (me_s + k) % sides
        send(
            mixed_out.at[to], mixed_in.at[me_s], mixed_send.at[k - 1], mixed_recv.at[k - 1], me_d, to
        )
    mixed_in[me_s] = mixed_out[me_s]
    for copy in small_copies[2:]:
        copy.wait()
    ids = ids_ref[...]
    levels = level_ref[...].astype(F32)
    expert_lane = lax.broadcasted_iota(jnp.int32, (rows, LANES), 1)
    spread = jnp.zeros((rows, LANES), F32)
    for k in range(ids.shape[1]):
        spread = spread + jnp.where(ids[:, k : k + 1] == expert_lane, levels[:, k : k + 1], 0.0)
    gathered[me_p, me_d, me_c, :, width:] = spread.astype(BF16)
    out_copy.wait()
    for k in range(1, sides):
        arrive(mixed_in.at[(me_s + sides - k) % sides], mixed_send.at[k - 1], mixed_recv.at[k - 1])
    features = jnp.concatenate([mixed_in[s].astype(F32) for s in range(sides)], axis=0)
    part = jnp.dot(features.astype(BF16), w_out[...], preferred_element_type=F32)
    part = part.reshape(sides, rows, width)
    part_own[...] = part
    part_out[...] = part.astype(BF16)
    for k in range(1, sides):
        to = (me_s + k) % sides
        send(part_out.at[to], part_in.at[k - 1], part_send.at[k - 1], part_recv.at[k - 1], me_d, to)
    stream = residual_ref[...].astype(F32) + part_own[me_s]
    for k in range(1, sides):
        arrive(part_in.at[k - 1], part_send.at[k - 1], part_recv.at[k - 1])
        stream = stream + part_in[k - 1].astype(F32)
    mean_square = jnp.mean(stream * stream, axis=1, keepdims=True)
    normed = stream * lax.rsqrt(mean_square + 1e-06) * gain_ref[...]
    gathered[me_p, me_d, me_c, :, :width] = normed.astype(BF16)

    def share(j, k, block):
        send(block, block, sib_send.at[j, k], sib_recv.at[j, k], me_d, sib_s)

    def across(k, block):
        for j in range(1, pairs):
            to = 2 * ((me_p + j) % pairs) + me_c
            send(block, block, across_send.at[j - 1, k], across_recv.at[j - 1, k], me_d, to)

    mine = gathered.at[me_p, me_d, me_c]
    for k in range(1, devs):
        send(mine, mine, dev_send.at[k - 1], dev_recv.at[k - 1], (me_d + k) % devs, me_s)
    across(0, mine)
    share(0, 0, mine)
    stream_ref[...] = stream.astype(BF16)
    for k in range(1, devs):
        block = gathered.at[me_p, (me_d + devs - k) % devs, me_c]
        arrive(block, dev_send.at[k - 1], dev_recv.at[k - 1])
        across(k, block)
        share(0, k, block)

    def from_sibling(j):
        for k in range(devs):
            block = gathered.at[(me_p + pairs - j) % pairs, (me_d + devs - k) % devs, 1 - me_c]
            arrive(block, sib_send.at[j, k], sib_recv.at[j, k])

    tokens = devs * 2 * rows
    expert = me_d * pairs + me_p
    token_lane = lax.broadcasted_iota(jnp.int32, (tokens, LANES), 1)

    def first_half(j, between=()):
        block = gathered[(me_p + pairs - j) % pairs, :, :, :, :width].astype(F32)
        block = block.reshape(tokens, width).astype(BF16)
        step = units // max(1, len(between))
        for i in range(units // step):
            cols = slice(i * step, (i + 1) * step)
            both = jnp.concatenate(
                [w_in[:, cols], w_in[:, units + i * step : units + (i + 1) * step]], axis=1
            )
            gate_up = jnp.dot(block, both, preferred_element_type=F32)
            gate = gate_up[:, :step]
            hidden[j, :, cols] = (gate / (1.0 + jnp.exp(-gate)) * gate_up[:, step:]).astype(BF16)
            if between:
                from_across(between[i])

    half = width // 2
    halves = (slice(0, half), slice(half, width))

    def second_half(j, c):
        level = gathered[(me_p + pairs - j) % pairs, :, :, :, width:].astype(F32)
        level = level.reshape(tokens, LANES)
        chosen = jnp.sum(jnp.where(token_lane == expert, level, 0.0), axis=1, keepdims=True)
        weight = chosen / jnp.sum(level, axis=1, keepdims=True)
        out = jnp.dot(hidden[j], w_down[:, halves[c]], preferred_element_type=F32) * weight
        out = out.reshape(devs, 2, rows, half)
        half_own[j, c] = jnp.where(me_c == 0, out[:, 0], out[:, 1])
        half_out[j, c] = jnp.where(me_c == 0, out[:, 1], out[:, 0]).astype(BF16)
        sems = half_send.at[j, c], half_recv.at[j, c]
        send(half_out.at[j, c], half_in.at[j, c], *sems, me_d, sib_s)

    def from_half(j):
        for c in range(2):
            arrive(half_in.at[j, c], half_send.at[j, c], half_recv.at[j, c])

    def joined(j, c, dev):
        return half_own[j, c, dev] + half_in[j, c, dev].astype(F32)

    def from_across(ks):
        for k in ks:
            for j in range(1, pairs):
                block = gathered.at[(me_p + pairs - j) % pairs, (me_d + devs - k) % devs, me_c]
                arrive(block, across_send.at[j - 1, k], across_recv.at[j - 1, k])
                share(j, k, block)

    in_copy.wait()
    order = list(range(devs))
    cuts = [order[: devs // 2], order[devs // 2 : devs * 3 // 4], order[devs * 3 // 4 : devs - 1]]
    from_across(cuts[0])
    from_sibling(0)
    first_half(0, (cuts[1], cuts[2], order[devs - 1 :]))
    down_copy.wait()
    for j in range(1, pairs):
        from_sibling(j)
        first_half(j)
        second_half(j, 0)
        second_half(j, 1)
    second_half(0, 0)

    for j in range(1, pairs):
        from_half(j)
        to = 2 * ((me_p + pairs - j) % pairs) + me_c
        for k in range(1, devs + 1):
            dev = (me_d + k) % devs
            for c in range(2):
                pair_out[j - 1, dev, :, halves[c]] = joined(j, c, dev).astype(BF16)
            sems = pair_send.at[j - 1, k - 1], pair_recv.at[j - 1, k - 1]
            send(pair_out.at[j - 1, dev], pair_in.at[j - 1, dev], *sems, me_d, to)
    second_half(0, 1)
    from_half(0)
    total = None
    for k in range(1, devs + 1):
        dev = (me_d + k) % devs
        total = jnp.concatenate([joined(0, c, dev) for c in range(2)], axis=1)
        for j in range(1, pairs):
            arrive(pair_in.at[j - 1, dev], pair_send.at[j - 1, k - 1], pair_recv.at[j - 1, k - 1])
            total = total + pair_in[j - 1, dev].astype(F32)
        if k < devs:
            last_out[k - 1] = total.astype(BF16)
            sems = last_send.at[k - 1], last_recv.at[k - 1]
            send(last_out.at[k - 1], last_in.at[k - 1], *sems, dev, me_s)
    for k in range(1, devs):
        arrive(last_in.at[k - 1], last_send.at[k - 1], last_recv.at[k - 1])
        total = total + last_in[k - 1].astype(F32)
    sum_ref[...] = total.astype(BF16)
    for copy in sent:
        copy.wait_send()


def body(
    queries,
    kv_cache,
    new_kv,
    lengths,
    residual,
    w_out,
    norm_gain,
    expert_ids,
    route_level,
    w_in,
    w_down,
):
    devs, sides = lax.axis_size("dev"), lax.axis_size("side")
    pairs = sides // 2
    rows, width = residual.shape
    heads = queries.shape[1] // HD
    units = w_down.shape[1]
    tokens = devs * 2 * rows
    dma = pltpu.SemaphoreType.DMA
    vmem = pl.BlockSpec(memory_space=pltpu.VMEM)
    hbm = pl.BlockSpec(memory_space=pl.ANY)
    norm_gain = norm_gain.reshape(1, -1)
    small = (queries, new_kv, residual, norm_gain, expert_ids, route_level)
    return pl.pallas_call(
        functools.partial(kernel, devs, sides),
        out_shape=(
            pltpu.VMEM((rows, width), BF16),
            pltpu.VMEM((rows, width), BF16),
        ),
        in_specs=[pl.BlockSpec(memory_space=pltpu.SMEM)] + [hbm] * 10,
        out_specs=(vmem, vmem),
        scratch_shapes=[
            *(pltpu.VMEM(x.shape, x.dtype) for x in small),
            pltpu.VMEM(kv_cache.shape, BF16),
            pltpu.VMEM(w_out.shape, BF16),
            pltpu.VMEM(w_in.shape[1:], BF16),
            pltpu.VMEM(w_down.shape[1:], BF16),
            pltpu.VMEM((rows * heads, HD), F32),
            pltpu.VMEM((sides, rows, w_out.shape[0]), BF16),
            pltpu.VMEM((sides, rows, w_out.shape[0]), BF16),
            pltpu.VMEM((sides, rows, width), BF16),
            pltpu.VMEM((sides - 1, rows, width), BF16),
            pltpu.VMEM((sides, rows, width), F32),
            pltpu.VMEM((pairs, devs, 2, rows, width + LANES), BF16),
            pltpu.VMEM((pairs, tokens, units), BF16),
            pltpu.VMEM((pairs, 2, devs, rows, width // 2), BF16),
            pltpu.VMEM((pairs, 2, devs, rows, width // 2), BF16),
            pltpu.VMEM((pairs, 2, devs, rows, width // 2), F32),
            pltpu.VMEM((max(1, pairs - 1), devs, rows, width), BF16),
            pltpu.VMEM((max(1, pairs - 1), devs, rows, width), BF16),
            pltpu.VMEM((devs - 1, rows, width), BF16),
            pltpu.VMEM((devs - 1, rows, width), BF16),
            dma((len(small),)),
            dma((rows,)),
            dma((3,)),
            dma((sides - 1,)),
            dma((sides - 1,)),
            dma((sides - 1,)),
            dma((sides - 1,)),
            dma((devs - 1,)),
            dma((devs - 1,)),
            dma((max(1, pairs - 1), devs)),
            dma((max(1, pairs - 1), devs)),
            dma((pairs, devs)),
            dma((pairs, devs)),
            dma((pairs, 2)),
            dma((pairs, 2)),
            dma((max(1, pairs - 1), devs)),
            dma((max(1, pairs - 1), devs)),
            dma((devs - 1,)),
            dma((devs - 1,)),
        ],
        compiler_params=pltpu.CompilerParams(
            collective_id=0, has_side_effects=True, vmem_limit_bytes=56 * 1024 * 1024
        ),
    )(
        lengths,
        *small,
        kv_cache,
        w_out,
        w_in,
        w_down,
    )


def solution(mesh):
    return jax.shard_map(
        body,
        mesh=mesh,
        in_specs=(
            P(("groups", "dev", "side"), None),
            P(("groups", "dev", "side"), None, None),
            P(("groups", "dev", "side"), None),
            P(("groups", "dev", "side")),
            P(("groups", "dev", "side"), None),
            P("side", None),
            P(),
            P(("groups", "dev", "side"), None),
            P(("groups", "dev", "side"), None),
            P(("dev", "side"), None, None),
            P(("dev", "side"), None, None),
        ),
        out_specs=(P(("groups", "dev", "side"), None), P(("groups", "dev", "side"), None)),
        check_vma=False,
    )
```

```python
import functools
import math

import jax
import jax.numpy as jnp
from jax import lax
from jax.experimental import pallas as pl
from jax.experimental.pallas import tpu as pltpu
from jax.sharding import PartitionSpec as P

HD = 128
LANES = 128
MESH = pl.DeviceIdType.MESH
F32 = jnp.float32
BF16 = jnp.bfloat16


def kernel(
    devs,
    sides,
    lengths_ref,
    queries_hbm,
    new_kv_hbm,
    residual_hbm,
    gain_hbm,
    ids_hbm,
    level_hbm,
    kv_hbm,
    w_out_hbm,
    w_in_hbm,
    w_down_hbm,
    stream_ref,
    sum_ref,
    queries_ref,
    new_kv_ref,
    residual_ref,
    gain_ref,
    ids_ref,
    level_ref,
    kv,
    w_out,
    w_in,
    w_down,
    by_head,
    mixed_out,
    mixed_in,
    part_out,
    part_in,
    part_own,
    gathered,
    hidden,
    half_out,
    half_in,
    half_own,
    pair_out,
    pair_in,
    last_out,
    last_in,
    small_sem,
    kv_sem,
    weight_sem,
    mixed_send,
    mixed_recv,
    part_send,
    part_recv,
    dev_send,
    dev_recv,
    across_send,
    across_recv,
    sib_send,
    sib_recv,
    half_send,
    half_recv,
    pair_send,
    pair_recv,
    last_send,
    last_recv,
):
    rows, width = residual_ref.shape
    cache = kv_hbm.shape[1]
    heads = queries_ref.shape[1] // HD
    split = new_kv_ref.shape[1] // 2
    kv_heads = split // HD
    group = heads // kv_heads
    side_heads = heads // sides
    pairs = sides // 2
    units = w_down_hbm.shape[1]
    me_d = lax.axis_index("dev")
    me_s = lax.axis_index("side")
    me_p, me_c = me_s // 2, me_s % 2
    sib_s = 2 * me_p + 1 - me_c
    sent = []

    def send(src, dst, send_sem, recv_sem, dev, side):
        copy = pltpu.make_async_remote_copy(
            src_ref=src,
            dst_ref=dst,
            send_sem=send_sem,
            recv_sem=recv_sem,
            device_id={"dev": dev, "side": side},
            device_id_type=MESH,
        )
        copy.start()
        sent.append(copy)

    def arrive(dst, send_sem, recv_sem):
        pltpu.make_async_remote_copy(
            src_ref=dst,
            dst_ref=dst,
            send_sem=send_sem,
            recv_sem=recv_sem,
            device_id={"dev": me_d, "side": sib_s},
            device_id_type=MESH,
        ).wait_recv()

    small = (
        (queries_hbm, queries_ref),
        (new_kv_hbm, new_kv_ref),
        (residual_hbm, residual_ref),
        (gain_hbm, gain_ref),
        (ids_hbm, ids_ref),
        (level_hbm, level_ref),
    )
    small_copies = [
        pltpu.make_async_copy(src, dst, small_sem.at[i]) for i, (src, dst) in enumerate(small)
    ]
    kv_copies = [pltpu.make_async_copy(kv_hbm.at[r], kv.at[r], kv_sem.at[r]) for r in range(rows)]
    for copy in small_copies[:2] + kv_copies + small_copies[2:]:
        copy.start()
    out_copy = pltpu.make_async_copy(w_out_hbm, w_out, weight_sem.at[0])
    in_copy = pltpu.make_async_copy(w_in_hbm.at[0], w_in, weight_sem.at[1])
    down_copy = pltpu.make_async_copy(w_down_hbm.at[0], w_down, weight_sem.at[2])
    out_copy.start()
    in_copy.start()
    down_copy.start()

    barrier = pltpu.get_barrier_semaphore()
    for k in range(1, sides):
        pl.semaphore_signal(
            barrier, inc=1, device_id={"side": (me_s + k) % sides}, device_id_type=MESH
        )
    for k in range(1, devs):
        pl.semaphore_signal(
            barrier, inc=1, device_id={"dev": (me_d + k) % devs}, device_id_type=MESH
        )

    small_copies[0].wait()
    small_copies[1].wait()
    for h in range(heads):
        by_head[pl.ds(h, rows, stride=heads), :] = queries_ref[:, h * HD : (h + 1) * HD].astype(F32)
    new_key = new_kv_ref[:, :split].astype(F32)
    new_value = new_kv_ref[:, split:].astype(F32)
    scaling = 1.0 / math.sqrt(HD)
    head_group = lax.broadcasted_iota(jnp.int32, (heads, split), 0) // group
    lane_group = lax.broadcasted_iota(jnp.int32, (heads, split), 1) // HD
    own_lanes = head_group == lane_group
    position = lax.broadcasted_iota(jnp.int32, (heads, cache), 1)
    wide = [
        jnp.where(
            own_lanes,
            jnp.concatenate([by_head[r * heads : (r + 1) * heads, :]] * kv_heads, axis=1),
            0.0,
        )
        for r in range(rows)
    ]
    own_score = [
        jnp.sum(wide[r] * new_key[r : r + 1, :], axis=1, keepdims=True) * scaling
        for r in range(rows)
    ]
    for copy in kv_copies:
        copy.wait()
    scores = [
        lax.dot_general(
            wide[r].astype(BF16),
            kv[r, :, :split],
            (((1,), (1,)), ((), ())),
            preferred_element_type=F32,
        )
        for r in range(rows)
    ]
    scores = [
        jnp.where(position < lengths_ref[r], scores[r] * scaling, -jnp.inf) for r in range(rows)
    ]
    peak = [
        jnp.maximum(jnp.max(scores[r], axis=1, keepdims=True), own_score[r]) for r in range(rows)
    ]
    weights = [jnp.exp(scores[r] - peak[r]) for r in range(rows)]
    own_weight = [jnp.exp(own_score[r] - peak[r]) for r in range(rows)]
    denominator = [
        jnp.sum(weights[r], axis=1, keepdims=True) + own_weight[r] for r in range(rows)
    ]
    probability = [(weights[r] / denominator[r]).astype(BF16) for r in range(rows)]
    own_prob = [(own_weight[r] / denominator[r]).astype(BF16).astype(F32) for r in range(rows)]
    mixed = [
        jnp.dot(probability[r], kv[r, :, split:], preferred_element_type=F32) for r in range(rows)
    ]
    for r in range(rows):
        whole = jnp.where(own_lanes, mixed[r] + own_prob[r] * new_value[r : r + 1, :], 0.0)
        narrow = whole[:, :HD]
        for g in range(1, kv_heads):
            narrow = narrow + whole[:, g * HD : (g + 1) * HD]
        by_head[r * heads : (r + 1) * heads, :] = narrow
    for s in range(sides):
        taken = [
            by_head[pl.ds(s * side_heads + h, rows, stride=heads), :] for h in range(side_heads)
        ]
        mixed_out[s] = jnp.concatenate(taken, axis=1).astype(BF16)

    pl.semaphore_wait(barrier, sides - 1 + devs - 1)
    for k in range(1, sides):
        to = (me_s + k) % sides
        send(
            mixed_out.at[to], mixed_in.at[me_s], mixed_send.at[k - 1], mixed_recv.at[k - 1], me_d, to
        )
    mixed_in[me_s] = mixed_out[me_s]
    for copy in small_copies[2:]:
        copy.wait()
    ids = ids_ref[...]
    levels = level_ref[...].astype(F32)
    expert_lane = lax.broadcasted_iota(jnp.int32, (rows, LANES), 1)
    spread = jnp.zeros((rows, LANES), F32)
    for k in range(ids.shape[1]):
        spread = spread + jnp.where(ids[:, k : k + 1] == expert_lane, levels[:, k : k + 1], 0.0)
    gathered[me_p, me_d, me_c, :, width:] = spread.astype(BF16)
    out_copy.wait()
    for k in range(1, sides):
        arrive(mixed_in.at[(me_s + sides - k) % sides], mixed_send.at[k - 1], mixed_recv.at[k - 1])
    features = jnp.concatenate([mixed_in[s].astype(F32) for s in range(sides)], axis=0)
    part = jnp.dot(features.astype(BF16), w_out[...], preferred_element_type=F32)
    part = part.reshape(sides, rows, width)
    part_own[...] = part
    part_out[...] = part.astype(BF16)
    for k in range(1, sides):
        to = (me_s + k) % sides
        send(part_out.at[to], part_in.at[k - 1], part_send.at[k - 1], part_recv.at[k - 1], me_d, to)
    stream = residual_ref[...].astype(F32) + part_own[me_s]
    for k in range(1, sides):
        arrive(part_in.at[k - 1], part_send.at[k - 1], part_recv.at[k - 1])
        stream = stream + part_in[k - 1].astype(F32)
    mean_square = jnp.mean(stream * stream, axis=1, keepdims=True)
    normed = stream * lax.rsqrt(mean_square + 1e-06) * gain_ref[...]
    gathered[me_p, me_d, me_c, :, :width] = normed.astype(BF16)

    def share(j, k, block):
        send(block, block, sib_send.at[j, k], sib_recv.at[j, k], me_d, sib_s)

    def across(k, block):
        for j in range(1, pairs):
            to = 2 * ((me_p + j) % pairs) + me_c
            send(block, block, across_send.at[j - 1, k], across_recv.at[j - 1, k], me_d, to)

    mine = gathered.at[me_p, me_d, me_c]
    for k in range(1, devs):
        send(mine, mine, dev_send.at[k - 1], dev_recv.at[k - 1], (me_d + k) % devs, me_s)
    across(0, mine)
    share(0, 0, mine)
    stream_ref[...] = stream.astype(BF16)
    for k in range(1, devs):
        block = gathered.at[me_p, (me_d + devs - k) % devs, me_c]
        arrive(block, dev_send.at[k - 1], dev_recv.at[k - 1])
        across(k, block)
        share(0, k, block)

    def from_sibling(j):
        for k in range(devs):
            block = gathered.at[(me_p + pairs - j) % pairs, (me_d + devs - k) % devs, 1 - me_c]
            arrive(block, sib_send.at[j, k], sib_recv.at[j, k])

    tokens = devs * 2 * rows
    expert = me_d * pairs + me_p
    token_lane = lax.broadcasted_iota(jnp.int32, (tokens, LANES), 1)

    def first_half(j, between=()):
        block = gathered[(me_p + pairs - j) % pairs, :, :, :, :width].astype(F32)
        block = block.reshape(tokens, width).astype(BF16)
        step = units // max(1, len(between))
        for i in range(units // step):
            cols = slice(i * step, (i + 1) * step)
            both = jnp.concatenate(
                [w_in[:, cols], w_in[:, units + i * step : units + (i + 1) * step]], axis=1
            )
            gate_up = jnp.dot(block, both, preferred_element_type=F32)
            gate = gate_up[:, :step]
            hidden[j, :, cols] = (gate / (1.0 + jnp.exp(-gate)) * gate_up[:, step:]).astype(BF16)
            if between:
                from_across(between[i])

    def second_half(j):
        level = gathered[(me_p + pairs - j) % pairs, :, :, :, width:].astype(F32)
        level = level.reshape(tokens, LANES)
        chosen = jnp.sum(jnp.where(token_lane == expert, level, 0.0), axis=1, keepdims=True)
        weight = chosen / jnp.sum(level, axis=1, keepdims=True)
        out = jnp.dot(hidden[j], w_down[...], preferred_element_type=F32) * weight
        out = out.reshape(devs, 2, rows, width)
        half_own[j] = jnp.where(me_c == 0, out[:, 0], out[:, 1])
        half_out[j] = jnp.where(me_c == 0, out[:, 1], out[:, 0]).astype(BF16)
        send(half_out.at[j], half_in.at[j], half_send.at[j], half_recv.at[j], me_d, sib_s)

    def from_across(ks):
        for k in ks:
            for j in range(1, pairs):
                block = gathered.at[(me_p + pairs - j) % pairs, (me_d + devs - k) % devs, me_c]
                arrive(block, across_send.at[j - 1, k], across_recv.at[j - 1, k])
                share(j, k, block)

    in_copy.wait()
    order = list(range(devs))
    cuts = [order[: devs // 2], order[devs // 2 : devs * 3 // 4], order[devs * 3 // 4 : devs - 1]]
    from_across(cuts[0])
    from_sibling(0)
    first_half(0, (cuts[1], cuts[2], order[devs - 1 :]))
    down_copy.wait()
    for j in range(1, pairs):
        from_sibling(j)
        first_half(j)
        second_half(j)
    second_half(0)

    far_first = sorted(range(1, devs), key=lambda k: -min(k, devs - k)) + [devs]
    for j in range(1, pairs):
        arrive(half_in.at[j], half_send.at[j], half_recv.at[j])
        to = 2 * ((me_p + pairs - j) % pairs) + me_c
        for k in far_first:
            dev = (me_d + k) % devs
            pair_out[j - 1, dev] = (half_own[j, dev] + half_in[j, dev].astype(F32)).astype(BF16)
            send(
                pair_out.at[j - 1, dev],
                pair_in.at[j - 1, dev],
                pair_send.at[j - 1, k - 1],
                pair_recv.at[j - 1, k - 1],
                me_d,
                to,
            )
    arrive(half_in.at[0], half_send.at[0], half_recv.at[0])
    total = None
    for k in far_first:
        dev = (me_d + k) % devs
        total = half_own[0, dev] + half_in[0, dev].astype(F32)
        for j in range(1, pairs):
            arrive(pair_in.at[j - 1, dev], pair_send.at[j - 1, k - 1], pair_recv.at[j - 1, k - 1])
            total = total + pair_in[j - 1, dev].astype(F32)
        if k < devs:
            last_out[k - 1] = total.astype(BF16)
            send(
                last_out.at[k - 1],
                last_in.at[k - 1],
                last_send.at[k - 1],
                last_recv.at[k - 1],
                dev,
                me_s,
            )
    for k in range(1, devs):
        arrive(last_in.at[k - 1], last_send.at[k - 1], last_recv.at[k - 1])
        total = total + last_in[k - 1].astype(F32)
    sum_ref[...] = total.astype(BF16)
    for copy in sent:
        copy.wait_send()


def body(
    queries,
    kv_cache,
    new_kv,
    lengths,
    residual,
    w_out,
    norm_gain,
    expert_ids,
    route_level,
    w_in,
    w_down,
):
    devs, sides = lax.axis_size("dev"), lax.axis_size("side")
    pairs = sides // 2
    rows, width = residual.shape
    heads = queries.shape[1] // HD
    units = w_down.shape[1]
    tokens = devs * 2 * rows
    dma = pltpu.SemaphoreType.DMA
    vmem = pl.BlockSpec(memory_space=pltpu.VMEM)
    hbm = pl.BlockSpec(memory_space=pl.ANY)
    norm_gain = norm_gain.reshape(1, -1)
    small = (queries, new_kv, residual, norm_gain, expert_ids, route_level)
    return pl.pallas_call(
        functools.partial(kernel, devs, sides),
        out_shape=(
            pltpu.VMEM((rows, width), BF16),
            pltpu.VMEM((rows, width), BF16),
        ),
        in_specs=[pl.BlockSpec(memory_space=pltpu.SMEM)] + [hbm] * 10,
        out_specs=(vmem, vmem),
        scratch_shapes=[
            *(pltpu.VMEM(x.shape, x.dtype) for x in small),
            pltpu.VMEM(kv_cache.shape, BF16),
            pltpu.VMEM(w_out.shape, BF16),
            pltpu.VMEM(w_in.shape[1:], BF16),
            pltpu.VMEM(w_down.shape[1:], BF16),
            pltpu.VMEM((rows * heads, HD), F32),
            pltpu.VMEM((sides, rows, w_out.shape[0]), BF16),
            pltpu.VMEM((sides, rows, w_out.shape[0]), BF16),
            pltpu.VMEM((sides, rows, width), BF16),
            pltpu.VMEM((sides - 1, rows, width), BF16),
            pltpu.VMEM((sides, rows, width), F32),
            pltpu.VMEM((pairs, devs, 2, rows, width + LANES), BF16),
            pltpu.VMEM((pairs, tokens, units), BF16),
            pltpu.VMEM((pairs, devs, rows, width), BF16),
            pltpu.VMEM((pairs, devs, rows, width), BF16),
            pltpu.VMEM((pairs, devs, rows, width), F32),
            pltpu.VMEM((max(1, pairs - 1), devs, rows, width), BF16),
            pltpu.VMEM((max(1, pairs - 1), devs, rows, width), BF16),
            pltpu.VMEM((devs - 1, rows, width), BF16),
            pltpu.VMEM((devs - 1, rows, width), BF16),
            dma((len(small),)),
            dma((rows,)),
            dma((3,)),
            dma((sides - 1,)),
            dma((sides - 1,)),
            dma((sides - 1,)),
            dma((sides - 1,)),
            dma((devs - 1,)),
            dma((devs - 1,)),
            dma((max(1, pairs - 1), devs)),
            dma((max(1, pairs - 1), devs)),
            dma((pairs, devs)),
            dma((pairs, devs)),
            dma((pairs,)),
            dma((pairs,)),
            dma((max(1, pairs - 1), devs)),
            dma((max(1, pairs - 1), devs)),
            dma((devs - 1,)),
            dma((devs - 1,)),
        ],
        compiler_params=pltpu.CompilerParams(
            collective_id=0, has_side_effects=True, vmem_limit_bytes=56 * 1024 * 1024
        ),
    )(
        lengths,
        *small,
        kv_cache,
        w_out,
        w_in,
        w_down,
    )


def solution(mesh):
    return jax.shard_map(
        body,
        mesh=mesh,
        in_specs=(
            P(("groups", "dev", "side"), None),
            P(("groups", "dev", "side"), None, None),
            P(("groups", "dev", "side"), None),
            P(("groups", "dev", "side")),
            P(("groups", "dev", "side"), None),
            P("side", None),
            P(),
            P(("groups", "dev", "side"), None),
            P(("groups", "dev", "side"), None),
            P(("dev", "side"), None, None),
            P(("dev", "side"), None, None),
        ),
        out_specs=(P(("groups", "dev", "side"), None), P(("groups", "dev", "side"), None)),
        check_vma=False,
    )
```
